256 devices in a mesh: gx: 32 (over y, x, core), gy: 8 (over z).
Axes of the slice: x: 4, y: 4, z: 8, core: 2. Of those that a mesh axis runs over, the one named last changes fastest.
Arguments:
- positions: float32 [3, 8388608], P(None, ('gx', 'gy')), may hold values from -0.5 to 1.5
- charges: float32 [8388608], P(('gx', 'gy')), may hold values from -0.09375 to 0.09375
- moment_freq: float32 [3, 121], replicated, may hold values from -2 to 2
- moment_phase: float32 [121], replicated, may hold values from -3.140625 to 3.140625
- m2l_ops: float32 [16, 121, 121], replicated, may hold values from -0.09375 to 0.09375
- child_parent_shift_matrix: float32 [8, 121, 121], replicated, may hold values from -0.1875 to 0.1875
- send_leaf: int32 [256, 256, 2], P(('gx', 'gy')), may hold values from 0 to 63
- send_count: int32 [256, 256], P(('gx', 'gy')), may hold values from 0 to 2, as said below
- far_src: int32 [16384, 32], P(('gx', 'gy')), may hold values from -1 to 575, as said below
- far_class: int32 [16384, 32], P(('gx', 'gy')), may hold values from 0 to 15
- near_src: int32 [16384, 8], P(('gx', 'gy')), may hold values from -1 to 575, as said below
- near_shift: int32 [16384, 8], P(('gx', 'gy')), may hold values from 0 to 26
- top_list: int32 [256, 32], P(('gx', 'gy')), may hold values from 0 to 255
- top_class: int32 [256, 32], P(('gx', 'gy')), may hold values from 0 to 15
Outputs:
- potential: float32 [8388608], P(('gx', 'gy'))
The draws below stay inside these ranges and needn't reach their ends.
Inputs may be any that keep to these rules, and one draw needn't show every extreme that they name: send_count[p, d] slots of sender p toward receiver d carry a leaf; the last device fills all 2 slots toward every receiver. `far_src`: an entry of leaf g on device d is -1 (padding), an own leaf i < 64, or 64 + p * 2 + s with s < send_count[p, d]. `near_src`: as for far_src; the first entry of each leaf is the leaf itself.
All inputs are finite; a program needn't handle non-finite values.
Results may differ from the reference program's by a relative error of at most 0.0003.
Values sent between devices are 32-bit elements; how exact they have to be, the bound alone decides.
A program may use at most 128 MiB of HBM per device.

```python
import math
import jax
import jax.numpy as jnp
from jax import lax

LEAF_DEV = 64
LEAF_BODIES = 512
NCOEF = 121
SLOTS = 2
FAR_LIST = 32
NEAR_LIST = 8
TOP_LIST = 32
OFFSET_CLASSES = 16
LEAVES = 16384
DEVICES = 256


def pair_counts(key):
    base = jax.random.randint(key, (DEVICES, DEVICES), 0, SLOTS + 1, dtype=jnp.int32)
    busiest = (jnp.arange(DEVICES, dtype=jnp.int32) == DEVICES - 1)[:, None]
    return jnp.where(busiest, SLOTS, base).astype(jnp.int32)


def pool_pointers(key, counts, columns, first_own):
    pieces = jax.random.split(key, 4)
    leaf_ids = jnp.arange(LEAVES, dtype=jnp.int32)
    owner_dev = (leaf_ids // LEAF_DEV)[:, None]
    sender = jax.random.randint(pieces[0], (LEAVES, columns), 0, DEVICES, dtype=jnp.int32)
    slot_pos = jax.random.randint(pieces[1], (LEAVES, columns), 0, SLOTS, dtype=jnp.int32)
    own_leaf = jax.random.randint(pieces[2], (LEAVES, columns), 0, LEAF_DEV, dtype=jnp.int32)
    chooser = jax.random.randint(pieces[3], (LEAVES, columns), 0, 4, dtype=jnp.int32)
    active_count = counts[sender, owner_dev]
    remote = jnp.where(slot_pos < active_count, LEAF_DEV + sender * SLOTS + slot_pos, -1)
    pointers = jnp.where(chooser == 0, own_leaf, remote)
    pointers = pointers.at[::LEAF_DEV, columns - 1].set(LEAF_DEV + DEVICES * SLOTS - 1)
    if first_own:
        pointers = pointers.at[:, 0].set(leaf_ids % LEAF_DEV)
    return pointers.astype(jnp.int32)


def draw_send_count(key, part):
    return pair_counts(key)


def draw_far_src(key, part):
    counts = pair_counts(key)
    key = jax.random.fold_in(key, 3)
    return pool_pointers(key, counts, FAR_LIST, False)


def draw_near_src(key, part):
    counts = pair_counts(key)
    key = jax.random.fold_in(key, 5)
    return pool_pointers(key, counts, NEAR_LIST, True)


def draw_positions(key, part):
    key = jax.random.fold_in(key, 7)
    pieces = jax.random.split(key, 1)
    shape = (3, LEAVES * LEAF_BODIES)
    spread = jax.random.uniform(pieces[0], shape, jnp.float32, -0.5, 1.5)
    return spread.astype(jnp.float32)


def draw_charges(key, part):
    key = jax.random.fold_in(key, 11)
    pieces = jax.random.split(key, 1)
    scale = (LEAF_BODIES * NEAR_LIST) ** (-0.5)
    rough = jax.random.truncated_normal(pieces[0], -6.0, 6.0, (LEAVES, LEAF_BODIES), jnp.float32)
    return (scale * rough).reshape(LEAVES * LEAF_BODIES).astype(jnp.float32)


def place_ends(values, stream_key, low, high):
    spot = [jax.random.randint(jax.random.fold_in(stream_key, axis), (), 0, length) for axis, length in enumerate(values.shape)]
    longest = values.shape.index(max(values.shape))
    neighbour = spot[:longest] + [(spot[longest] + 1) % values.shape[longest]] + spot[longest + 1:]
    return values.at[tuple(spot)].set(low).at[tuple(neighbour)].set(high)


def centred(rng, dims, width, reach, held_as=jnp.bfloat16):
    entries = jax.random.normal(rng, dims, jnp.float32) * width
    return jnp.minimum(jnp.maximum(entries, -reach), reach).astype(held_as)


def setup_inputs(seed: int = 0) -> dict:
    splits = jax.random.split(jax.random.key(seed), 15)
    return {
        "positions": draw_positions(jax.random.fold_in(splits[14], 71), 0),
        "charges": draw_charges(jax.random.fold_in(splits[14], 71), 0),
        "moment_freq": jnp.clip(jax.random.uniform(splits[2], (3, NCOEF), jnp.float32, -2.0, 2.0), -2.0, 2.0),
        "moment_phase": jnp.clip(jax.random.uniform(splits[3], (NCOEF,), jnp.float32, -3.140625, 3.140625), -3.140625, 3.140625),
        "m2l_ops": centred(splits[4], (OFFSET_CLASSES, NCOEF, NCOEF), (NCOEF * FAR_LIST) ** -0.5, 0.09375, jnp.float32),
        "child_parent_shift_matrix": centred(splits[5], (8, NCOEF, NCOEF), (NCOEF * 8) ** -0.5, 0.1875, jnp.float32),
        "send_leaf": place_ends(jax.random.randint(splits[6], (DEVICES, DEVICES, SLOTS), 0, LEAF_DEV), jax.random.fold_in(splits[6], 1), 0, LEAF_DEV - 1).astype(jnp.int32),
        "send_count": draw_send_count(jax.random.fold_in(splits[14], 71), 0),
        "far_src": draw_far_src(jax.random.fold_in(splits[14], 71), 0),
        "far_class": place_ends(jax.random.randint(splits[9], (LEAVES, FAR_LIST), 0, OFFSET_CLASSES), jax.random.fold_in(splits[9], 1), 0, OFFSET_CLASSES - 1).astype(jnp.int32),
        "near_src": draw_near_src(jax.random.fold_in(splits[14], 71), 0),
        "near_shift": place_ends(jax.random.randint(splits[11], (LEAVES, NEAR_LIST), 0, 27), jax.random.fold_in(splits[11], 1), 0, 26).astype(jnp.int32),
        "top_list": place_ends(jax.random.randint(splits[12], (DEVICES, TOP_LIST), 0, DEVICES), jax.random.fold_in(splits[12], 1), 0, DEVICES - 1).astype(jnp.int32),
        "top_class": place_ends(jax.random.randint(splits[13], (DEVICES, TOP_LIST), 0, OFFSET_CLASSES), jax.random.fold_in(splits[13], 1), 0, OFFSET_CLASSES - 1).astype(jnp.int32),
    }


TWO_PI = 2.0 * math.pi
SOFTENING = 0.01
EXACT_PRECISION = lax.Precision.HIGHEST

def features(place, moment_freq, moment_phase):
    phase_arg = moment_freq[0][:, None] * place[0][None, :] + moment_freq[1][:, None] * place[1][None, :] + moment_freq[2][:, None] * place[2][None, :]
    return jnp.cos(TWO_PI * phase_arg + moment_phase[:, None])

def class_table(classes, number):
    return (classes[..., None] == jnp.arange(number, dtype=jnp.int32)).astype(jnp.float32)

def offset_vector(shift_class_index):
    return ((shift_class_index % 3 - 1).astype(jnp.float32), (shift_class_index // 3 % 3 - 1).astype(jnp.float32), (shift_class_index // 9 - 1).astype(jnp.float32))

def near_block(target_bodies, sources, weights, shift_class_index):
    accumulated = jnp.zeros((target_bodies.shape[0], target_bodies.shape[2]), jnp.float32)
    for column in range(sources.shape[1]):
        source = sources[:, column]
        shift_x, shift_y, shift_z = offset_vector(shift_class_index[:, column])
        delta_x = target_bodies[:, 0, :, None] - (source[:, 0, None, :] + shift_x[:, None, None])
        delta_y = target_bodies[:, 1, :, None] - (source[:, 1, None, :] + shift_y[:, None, None])
        delta_z = target_bodies[:, 2, :, None] - (source[:, 2, None, :] + shift_z[:, None, None])
        radius = delta_x * delta_x + delta_y * delta_y + delta_z * delta_z + SOFTENING
        summed = lax.optimization_barrier(jnp.sum(source[:, 3, None, :] * lax.rsqrt(radius), axis=2))
        accumulated = accumulated + summed * weights[:, column, None]
    return accumulated

def resolve(pointers, send_leaf, send_count):
    leaf_ids = jnp.arange(LEAVES, dtype=jnp.int32)
    owner_dev = (leaf_ids // LEAF_DEV)[:, None]
    clamped = jnp.maximum(pointers, 0)
    is_own = clamped < LEAF_DEV
    remote = jnp.maximum(clamped - LEAF_DEV, 0)
    sender = remote // SLOTS
    slot_pos = remote % SLOTS
    sent_leaf = send_leaf[sender, owner_dev, slot_pos]
    live_slot = slot_pos < send_count[sender, owner_dev]
    global_ids = jnp.where(is_own, owner_dev * LEAF_DEV + clamped, sender * LEAF_DEV + sent_leaf)
    usable = (pointers >= 0) & (is_own | live_slot)
    return (global_ids.astype(jnp.int32), usable.astype(jnp.float32))

def reference(positions, charges, moment_freq, moment_phase, m2l_ops, child_parent_shift_matrix, send_leaf, send_count, far_src, far_class, near_src, near_shift, top_list, top_class):
    block_pos = positions.reshape(3, DEVICES, LEAF_DEV * LEAF_BODIES).transpose(1, 0, 2)
    block_charge = charges.reshape(DEVICES, LEAF_DEV, LEAF_BODIES)

    def moment_step(inputs):
        place, charge_rows = inputs
        harmonic = features(place, moment_freq, moment_phase).reshape(NCOEF, LEAF_DEV, LEAF_BODIES)
        return jnp.einsum('klb,lb->lk', harmonic, charge_rows, precision=EXACT_PRECISION)
    moments = lax.map(moment_step, (block_pos, block_charge))
    grouped_moments = moments.reshape(DEVICES, LEAF_DEV // 8, 8, NCOEF).sum(axis=1)
    tops = jnp.einsum('cij,dcj->di', child_parent_shift_matrix, grouped_moments, precision=EXACT_PRECISION)
    picked = tops[top_list]
    top_grouped = jnp.einsum('dec,dej->dcj', class_table(top_class, OFFSET_CLASSES), picked, precision=EXACT_PRECISION)
    root_local_expansion = jnp.einsum('cij,dcj->di', m2l_ops, top_grouped, precision=EXACT_PRECISION)
    downward_sweep = jnp.einsum('hsw,ns->nhw', child_parent_shift_matrix, root_local_expansion, precision=EXACT_PRECISION)
    flat_moments = moments.reshape(LEAVES, NCOEF)
    leaf_bodies = jnp.concatenate([positions, charges[None, :]], axis=0).reshape(4, LEAVES, LEAF_BODIES).transpose(1, 0, 2)
    far_ids, far_usable = resolve(far_src, send_leaf, send_count)
    vectors = flat_moments[far_ids] * far_usable[..., None]
    grouped = jnp.einsum('lec,lej->lcj', class_table(far_class, OFFSET_CLASSES), vectors, precision=EXACT_PRECISION)
    local_exp = jnp.einsum('cij,lcj->li', m2l_ops, grouped, precision=EXACT_PRECISION)
    local_exp = local_exp.reshape(DEVICES, LEAF_DEV // 8, 8, NCOEF) + downward_sweep[:, None]
    local_exp = local_exp.reshape(DEVICES, LEAF_DEV, NCOEF)

    def far_step(inputs):
        place, expansion = inputs
        harmonic = features(place, moment_freq, moment_phase).reshape(NCOEF, LEAF_DEV, LEAF_BODIES)
        return jnp.einsum('klb,lk->lb', harmonic, expansion, precision=EXACT_PRECISION)
    far_field = lax.map(far_step, (block_pos, local_exp))
    near_ids, near_usable = resolve(near_src, send_leaf, send_count)

    def near_step(inputs):
        target_bodies, pointers, weights, shift_class_index = inputs
        return near_block(target_bodies, leaf_bodies[pointers], weights, shift_class_index)
    near_field = lax.map(near_step, (leaf_bodies[:, :3].reshape(LEAVES // 8, 8, 3, LEAF_BODIES), near_ids.reshape(LEAVES // 8, 8, NEAR_LIST), near_usable.reshape(LEAVES // 8, 8, NEAR_LIST), near_shift.reshape(LEAVES // 8, 8, NEAR_LIST)))
    return near_field.reshape(LEAVES * LEAF_BODIES) + far_field.reshape(LEAVES * LEAF_BODIES)
```

```python
import functools
import math

import jax
import jax.numpy as jnp
from jax import lax
from jax.experimental import pallas as pl
from jax.experimental.pallas import tpu as pltpu
from jax.sharding import PartitionSpec as P

F32 = jnp.float32
BF16 = jnp.bfloat16
SOFTENING = 0.01
LEAVES = 64
WIDTH = 512
KPAD = 128
GROUPS = 48
UNROLL = 8
COS = (1.0, -19.73920440673828, 64.93911743164062, -85.45011138916016, 60.16743087768555, -25.96688461303711, 6.527706146240234)


def split2(a):
    high = a.astype(BF16)
    return high, (a - high.astype(F32)).astype(BF16)


def split3(a):
    high = a.astype(BF16).astype(F32)
    rest = a - high
    middle = rest.astype(BF16).astype(F32)
    return high, middle, rest - middle


def dot_nt(a, b):
    return lax.dot_general(a, b, (((1,), (1,)), ((), ())), preferred_element_type=F32)


def dot_nn(a, b):
    return jnp.dot(a, b, preferred_element_type=F32)


def dot3(dot, a, b):
    a_high, a_low = split2(a)
    b_high, b_low = split2(b)
    return dot(a_high, b_high) + (dot(a_high, b_low) + dot(a_low, b_high))


def pad8(record):
    return jnp.concatenate([record, jnp.zeros((4, record.shape[1]), F32)], axis=0)


def right_side(body, centre):
    row = lax.broadcasted_iota(jnp.int32, body.shape, 0)
    point = jnp.where(row < 3, body - centre, 0.0)
    norm = jnp.sum(point * point, axis=0, keepdims=True) + SOFTENING
    high, middle, low = split3(jnp.where(row == 3, norm, -2.0 * point))
    high_one = jnp.where(row == 3, 1.0, high)
    middle_one = jnp.where(row == 3, 1.0, middle)
    return jnp.concatenate([high, middle, high_one, low, high_one, middle_one], axis=0).astype(BF16)


def left_side(body):
    row = lax.broadcasted_iota(jnp.int32, body.shape, 0)
    point = jnp.where(row < 3, body - 0.5, 0.0)
    norm = jnp.sum(point * point, axis=0, keepdims=True)
    high, middle, low = split3(jnp.where(row == 3, norm, point))
    one = jnp.where(row == 3, 1.0, high)
    return jnp.concatenate(
        [
            one,
            one,
            jnp.where(row == 3, high, middle),
            one,
            jnp.where(row == 3, middle, low),
            jnp.where(row == 3, low, middle),
        ],
        axis=0,
    )


def phase_weights(waves):
    waves = pad8(waves)
    row = lax.broadcasted_iota(jnp.int32, waves.shape, 0)
    freq = jnp.where(row < 3, waves, 0.0)
    turn = jnp.sum(jnp.where(row < 3, 0.5 * waves, waves), axis=0, keepdims=True)
    turn = turn - jnp.round(turn)
    high, middle, low = split3(jnp.where(row == 3, turn, -0.5 * freq))
    plain = jnp.where(row == 3, 0.0, high)
    groups = jnp.concatenate(
        [
            plain,
            plain,
            jnp.where(row == 3, high, middle),
            plain,
            jnp.where(row == 3, middle, low),
            jnp.where(row == 3, low, middle),
        ],
        axis=0,
    )
    return groups.T.astype(BF16)


def cosine_turns(turns):
    rest = turns - jnp.round(turns)
    square = rest * rest
    value = jnp.full_like(square, COS[-1])
    for coefficient in COS[-2::-1]:
        value = value * square + coefficient
    return value


def lane_fold(a):
    return (a[:, :128] + a[:, 128:256]) + (a[:, 256:384] + a[:, 384:])


def basis_leaf(body, weights):
    return cosine_turns(dot_nn(weights, right_side(body, 0.5)))


def upward(moments, shift_ref):
    grouped = moments.reshape(8, 8, KPAD).sum(axis=0)
    row = lax.broadcasted_iota(jnp.int32, grouped.shape, 0)
    total = jnp.zeros((8, KPAD), F32)
    for child in range(8):
        total = total + dot3(dot_nt, jnp.where(row == child, grouped, 0.0), shift_ref[child])
    return jnp.sum(total, axis=0, keepdims=True)


def feature_kernel(bodies, waves, shift, harmonic, left, moments, top, transposed):
    weights = phase_weights(waves[...])
    lane = lax.broadcasted_iota(jnp.int32, (KPAD, KPAD), 1)
    transposed[...] = jnp.zeros_like(transposed)

    def step(pair, carry):
        for half in range(2):
            leaf = pair * 2 + half
            body = pad8(bodies[leaf])
            basis = basis_leaf(body, weights)
            harmonic[leaf] = basis
            column = jnp.sum(lane_fold(basis * body[3:4]), axis=1, keepdims=True)
            transposed[...] = jnp.where(lane == leaf, column, transposed[...])
            left[leaf, :, :GROUPS] = left_side(body).T.astype(BF16)
        return carry

    lax.fori_loop(0, LEAVES // 2, step, 0)
    own = transposed[...].T[:LEAVES]
    moments[...] = own
    top[...] = jnp.broadcast_to(upward(own, shift), (8, KPAD))


def offset_vector(code):
    return (
        (code % 3 - 1).astype(F32),
        (code // 3 % 3 - 1).astype(F32),
        (code // 9 - 1).astype(F32),
    )


def source_right(body, shift):
    row = lax.broadcasted_iota(jnp.int32, body.shape, 0)
    shift_x, shift_y, shift_z = offset_vector(shift)
    centre = 0.5 - jnp.where(row == 0, shift_x, jnp.where(row == 1, shift_y, shift_z))
    return right_side(body, centre)


def pair_rows(left, right, charge, start, size):
    value = charge * lax.rsqrt(dot_nn(left[start : start + size], right))
    return lane_fold(value)


def local_expansions(pool_moments, m2l, shift, table, far_index, top_class, expansions):
    rows = pool_moments.shape[0]
    pool_high, pool_low = split2(pool_moments[...])
    for pair in range(8):
        op_high, op_low = split2(m2l[2 * pair : 2 * pair + 2].reshape(256, KPAD))
        moved = dot_nt(pool_high, op_high) + (dot_nt(pool_high, op_low) + dot_nt(pool_low, op_high))
        table[2 * pair * rows : (2 * pair + 1) * rows] = moved[:, :KPAD]
        table[(2 * pair + 1) * rows : (2 * pair + 2) * rows] = moved[:, KPAD:]
    table[16 * rows : 16 * rows + 8] = jnp.zeros((8, KPAD), F32)

    def tree(parts):
        while len(parts) > 1:
            parts = [a + b for a, b in zip(parts[::2], parts[1::2])]
        return parts[0]

    top_local = tree(
        [table[pl.ds(top_class[e] * rows + (rows - 32 + e), 1), :] for e in range(32)]
    )
    top_rows = jnp.broadcast_to(top_local, (8, KPAD))
    row = lax.broadcasted_iota(jnp.int32, (8, KPAD), 0)
    down = jnp.zeros((8, KPAD), F32)
    for child in range(8):
        down = jnp.where(row == child, dot3(dot_nn, top_rows, shift[child]), down)

    def gather(leaf, carry):
        base = leaf * 32
        expansions[pl.ds(leaf, 1), :] = tree(
            [table[pl.ds(far_index[base + e], 1), :] for e in range(32)]
        )
        return carry

    lax.fori_loop(0, LEAVES, gather, 0)
    return (expansions[...].reshape(8, 8, KPAD) + down[None]).reshape(LEAVES, KPAD)


def finish_kernel(
    count, codes, far_index, top_list, top_class,
    left, m2l, shift, own_moments, in_moments, tops,
    harmonic_hbm, bodies_hbm, in_bodies_hbm,
    out,
    pool, harmonic, near, pool_moments, table, expansions, sems,
):
    slots = in_bodies_hbm.shape[0]
    copy_own = pltpu.make_async_copy(bodies_hbm, pool.at[pl.ds(0, LEAVES)], sems.at[0])
    copy_in = pltpu.make_async_copy(in_bodies_hbm, pool.at[pl.ds(LEAVES, slots)], sems.at[1])
    copy_harmonic = pltpu.make_async_copy(harmonic_hbm, harmonic, sems.at[2])
    copy_own.start()
    copy_in.start()
    copy_harmonic.start()
    near[...] = jnp.zeros_like(near)
    rows = LEAVES + slots
    pool_moments[:LEAVES] = own_moments[...]
    pool_moments[LEAVES:rows] = in_moments[...]
    for e in range(32):
        pool_moments[rows + e : rows + e + 1, :] = tops[pl.ds(top_list[e], 1), :]
    local = local_expansions(pool_moments, m2l, shift, table, far_index, top_class, expansions)
    local_columns = jnp.concatenate([local, jnp.zeros((KPAD - LEAVES, KPAD), F32)], axis=0).T

    copy_own.wait()
    copy_in.wait()

    def near_step(group, carry):
        for member in range(UNROLL):
            code = codes[group * UNROLL + member]
            target = code & 63
            source = (code >> 6) & 1023
            live = (code >> 21).astype(F32)
            body = pad8(pool[source])
            right = source_right(body, (code >> 16) & 31)
            charge = body[3:4] * live
            for start in range(0, WIDTH, 128):
                near[target, start : start + 128] += pair_rows(
                    left.at[target][:, :GROUPS], right, charge, start, 128
                )
        return carry

    lax.fori_loop(0, (count[0] + UNROLL - 1) // UNROLL, near_step, 0)
    copy_harmonic.wait()
    ones = jnp.ones((8, 128), BF16)

    def far_step(group, columns):
        for member in range(8):
            leaf = group * 8 + member
            product = harmonic[leaf] * columns[:, member : member + 1]
            far = jnp.sum(product, axis=0, keepdims=True)
            near_high, near_low = split2(near[leaf])
            total = dot_nt(ones, near_high) + dot_nt(ones, near_low)
            out[pl.ds(leaf, 1), :] = total[:1] + far
        return pltpu.roll(columns, KPAD - 8, 1)

    lax.fori_loop(0, LEAVES // 8, far_step, local_columns)


def near_codes(near_src, near_shift, wanted):
    number = near_src.size
    flat = near_src.reshape(number)
    entry = jnp.arange(number, dtype=jnp.int32)
    code = (entry // near_src.shape[1]) + flat * 64 + near_shift.reshape(number) * 65536 + (1 << 21)
    wanted = wanted.reshape(number)
    place = jnp.sum(wanted[None, :] & (entry[None, :] < entry[:, None]), axis=1, dtype=jnp.int32)
    place = jnp.where(wanted, place, -1)
    codes = jnp.sum(jnp.where(place[None, :] == entry[:, None], code[None, :], 0), axis=1)
    return codes, jnp.sum(wanted, dtype=jnp.int32)[None]


SMEM = pl.BlockSpec(memory_space=pltpu.SMEM)
VMEM = pl.BlockSpec(memory_space=pltpu.VMEM)
ANY = pl.BlockSpec(memory_space=pl.ANY)


def pad_ops(ops):
    return jnp.pad(ops, ((0, 0), (0, KPAD - ops.shape[1]), (0, KPAD - ops.shape[2])))


def wave_rows(moment_freq, moment_phase):
    rows = jnp.concatenate([moment_freq, moment_phase[None] * (0.5 / math.pi)], axis=0)
    return jnp.pad(rows, ((0, 0), (0, KPAD - rows.shape[1])))


def run_features(bodies, waves, shift):
    return pl.pallas_call(
        feature_kernel,
        out_shape=[
            jax.ShapeDtypeStruct((LEAVES, KPAD, WIDTH), F32),
            jax.ShapeDtypeStruct((LEAVES, WIDTH, 128), BF16),
            jax.ShapeDtypeStruct((LEAVES, KPAD), F32),
            jax.ShapeDtypeStruct((8, KPAD), F32),
        ],
        in_specs=[VMEM] * 3,
        out_specs=[VMEM] * 4,
        scratch_shapes=[pltpu.VMEM((KPAD, KPAD), F32)],
        compiler_params=pltpu.CompilerParams(vmem_limit_bytes=60 << 20),
        cost_estimate=pl.CostEstimate(flops=20_000_000_000, bytes_accessed=30_000_000, transcendentals=0),
    )(bodies, waves, shift)


def run_finish(count, codes, far_index, top_list, top_class, left, m2l, shift, moments, in_moments, tops, harmonic, bodies, in_bodies):
    slots = in_bodies.shape[0]
    rows = LEAVES + slots + 32
    return pl.pallas_call(
        finish_kernel,
        out_shape=jax.ShapeDtypeStruct((LEAVES, WIDTH), F32),
        in_specs=[SMEM] * 5 + [VMEM] * 6 + [ANY] * 3,
        out_specs=VMEM,
        scratch_shapes=[
            pltpu.VMEM((LEAVES + slots, 4, WIDTH), F32),
            pltpu.VMEM((LEAVES, KPAD, WIDTH), F32),
            pltpu.VMEM((LEAVES, WIDTH, 128), F32),
            pltpu.VMEM((rows, KPAD), F32),
            pltpu.VMEM((16 * rows + 8, KPAD), F32),
            pltpu.VMEM((LEAVES, KPAD), F32),
            pltpu.SemaphoreType.DMA((3,)),
        ],
        compiler_params=pltpu.CompilerParams(vmem_limit_bytes=62 << 20),
        cost_estimate=pl.CostEstimate(flops=60_000_000_000, bytes_accessed=40_000_000, transcendentals=0),
    )(count, codes, far_index, top_list, top_class, left, m2l, shift, moments, in_moments, tops, harmonic, bodies, in_bodies)


def exchange(values):
    values = lax.all_to_all(values, "gx", split_axis=0, concat_axis=0, tiled=True)
    return lax.all_to_all(values, "gy", split_axis=1, concat_axis=1, tiled=True)


def local(
    positions,
    charges,
    moment_freq,
    moment_phase,
    m2l_ops,
    child_parent_shift_matrix,
    send_leaf,
    send_count,
    far_src,
    far_class,
    near_src,
    near_shift,
    top_list,
    top_class,
):
    leaves = far_src.shape[0]
    peers, slot_count = send_leaf.shape[1:]
    coarse_size = lax.axis_size("gx")
    fine_size = lax.axis_size("gy")
    bodies = (
        jnp.concatenate([positions, charges[None, :]], axis=0)
        .reshape(4, leaves, WIDTH)
        .transpose(1, 0, 2)
    )
    chosen = send_leaf[0]
    in_bodies = exchange(
        bodies[chosen].reshape(coarse_size, fine_size, slot_count, 4, WIDTH)
    ).reshape(peers * slot_count, 4, WIDTH)
    waves = wave_rows(moment_freq, moment_phase)
    shift = pad_ops(child_parent_shift_matrix)
    m2l = pad_ops(m2l_ops)
    harmonic, left, moments, top = run_features(bodies, waves, shift)
    sent = jnp.concatenate(
        [moments[chosen], jnp.broadcast_to(top[:1][None], (peers, 1, KPAD))], axis=1
    )
    came = exchange(sent.reshape(coarse_size, fine_size, slot_count + 1, KPAD)).reshape(
        peers, slot_count + 1, KPAD
    )
    in_moments = came[:, :slot_count].reshape(peers * slot_count, KPAD)
    tops = came[:, slot_count]
    codes, count = near_codes(near_src, near_shift, near_src >= 0)
    rows = leaves + peers * slot_count + 32
    far_index = jnp.where(far_src >= 0, far_class * rows + far_src, 16 * rows).reshape(-1)
    result = run_finish(
        count, codes, far_index, top_list[0], top_class[0], left, m2l, shift,
        moments, in_moments, tops, harmonic, bodies, in_bodies,
    )
    return result.reshape(leaves * WIDTH)


def solution(mesh):
    placed = (
        P(None, ("gx", "gy")),
        P(("gx", "gy")),
        P(),
        P(),
        P(),
        P(),
        P(("gx", "gy"), None, None),
        P(("gx", "gy"), None),
        P(("gx", "gy"), None),
        P(("gx", "gy"), None),
        P(("gx", "gy"), None),
        P(("gx", "gy"), None),
        P(("gx", "gy"), None),
        P(("gx", "gy"), None),
    )
    return jax.shard_map(
        local, mesh=mesh, in_specs=placed, out_specs=P(("gx", "gy")), check_vma=False
    )
```

```python
import functools
import math

import jax
import jax.numpy as jnp
from jax import lax
from jax.experimental import pallas as pl
from jax.experimental.pallas import tpu as pltpu
from jax.sharding import PartitionSpec as P

F32 = jnp.float32
BF16 = jnp.bfloat16
SOFTENING = 0.01
LEAVES = 64
WIDTH = 512
KPAD = 128
GROUPS = 48
UNROLL = 8
COS = (1.0, -19.73920440673828, 64.93911743164062, -85.45011138916016, 60.16743087768555, -25.96688461303711, 6.527706146240234)


def split2(a):
    high = a.astype(BF16)
    return high, (a - high.astype(F32)).astype(BF16)


def split3(a):
    high = a.astype(BF16).astype(F32)
    rest = a - high
    middle = rest.astype(BF16).astype(F32)
    return high, middle, rest - middle


def dot_nt(a, b):
    return lax.dot_general(a, b, (((1,), (1,)), ((), ())), preferred_element_type=F32)


def dot_nn(a, b):
    return jnp.dot(a, b, preferred_element_type=F32)


def dot3(dot, a, b):
    a_high, a_low = split2(a)
    b_high, b_low = split2(b)
    return dot(a_high, b_high) + (dot(a_high, b_low) + dot(a_low, b_high))


def pad8(record):
    return jnp.concatenate([record, jnp.zeros((4, record.shape[1]), F32)], axis=0)


def right_side(body, centre):
    row = lax.broadcasted_iota(jnp.int32, body.shape, 0)
    point = jnp.where(row < 3, body - centre, 0.0)
    norm = jnp.sum(point * point, axis=0, keepdims=True) + SOFTENING
    high, middle, low = split3(jnp.where(row == 3, norm, -2.0 * point))
    high_one = jnp.where(row == 3, 1.0, high)
    middle_one = jnp.where(row == 3, 1.0, middle)
    return jnp.concatenate([high, middle, high_one, low, high_one, middle_one], axis=0).astype(BF16)


def left_side(body):
    row = lax.broadcasted_iota(jnp.int32, body.shape, 0)
    point = jnp.where(row < 3, body - 0.5, 0.0)
    norm = jnp.sum(point * point, axis=0, keepdims=True)
    high, middle, low = split3(jnp.where(row == 3, norm, point))
    one = jnp.where(row == 3, 1.0, high)
    return jnp.concatenate(
        [
            one,
            one,
            jnp.where(row == 3, high, middle),
            one,
            jnp.where(row == 3, middle, low),
            jnp.where(row == 3, low, middle),
        ],
        axis=0,
    )


def phase_weights(waves):
    waves = pad8(waves)
    row = lax.broadcasted_iota(jnp.int32, waves.shape, 0)
    freq = jnp.where(row < 3, waves, 0.0)
    turn = jnp.sum(jnp.where(row < 3, 0.5 * waves, waves), axis=0, keepdims=True)
    turn = turn - jnp.round(turn)
    high, middle, low = split3(jnp.where(row == 3, turn, -0.5 * freq))
    plain = jnp.where(row == 3, 0.0, high)
    groups = jnp.concatenate(
        [
            plain,
            plain,
            jnp.where(row == 3, high, middle),
            plain,
            jnp.where(row == 3, middle, low),
            jnp.where(row == 3, low, middle),
        ],
        axis=0,
    )
    return groups.T.astype(BF16)


def cosine_turns(turns):
    rest = turns - jnp.round(turns)
    square = rest * rest
    value = jnp.full_like(square, COS[-1])
    for coefficient in COS[-2::-1]:
        value = value * square + coefficient
    return value


def lane_fold(a):
    return (a[:, :128] + a[:, 128:256]) + (a[:, 256:384] + a[:, 384:])


def basis_leaf(body, weights):
    return cosine_turns(dot_nn(weights, right_side(body, 0.5)))


def upward(moments, shift_ref):
    grouped = moments.reshape(8, 8, KPAD).sum(axis=0)
    row = lax.broadcasted_iota(jnp.int32, grouped.shape, 0)
    total = jnp.zeros((8, KPAD), F32)
    for child in range(8):
        total = total + dot3(dot_nt, jnp.where(row == child, grouped, 0.0), shift_ref[child])
    return jnp.sum(total, axis=0, keepdims=True)


def offset_vector(code):
    return (
        (code % 3 - 1).astype(F32),
        (code // 3 % 3 - 1).astype(F32),
        (code // 9 - 1).astype(F32),
    )


def source_right(body, shift):
    row = lax.broadcasted_iota(jnp.int32, body.shape, 0)
    shift_x, shift_y, shift_z = offset_vector(shift)
    centre = 0.5 - jnp.where(row == 0, shift_x, jnp.where(row == 1, shift_y, shift_z))
    return right_side(body, centre)


def pair_rows(left, right, charge, start, size):
    value = charge * lax.rsqrt(dot_nn(left[start : start + size], right))
    return lane_fold(value)


def local_expansions(pool_moments, m2l, shift, table, far_index, top_class, expansions):
    rows = pool_moments.shape[0]
    pool_high, pool_low = split2(pool_moments[...])
    for pair in range(8):
        op_high, op_low = split2(m2l[2 * pair : 2 * pair + 2].reshape(256, KPAD))
        moved = dot_nt(pool_high, op_high) + (dot_nt(pool_high, op_low) + dot_nt(pool_low, op_high))
        table[2 * pair * rows : (2 * pair + 1) * rows] = moved[:, :KPAD]
        table[(2 * pair + 1) * rows : (2 * pair + 2) * rows] = moved[:, KPAD:]
    table[16 * rows : 16 * rows + 8] = jnp.zeros((8, KPAD), F32)

    def tree(parts):
        while len(parts) > 1:
            parts = [a + b for a, b in zip(parts[::2], parts[1::2])]
        return parts[0]

    top_local = tree(
        [table[pl.ds(top_class[e] * rows + (rows - 32 + e), 1), :] for e in range(32)]
    )
    top_rows = jnp.broadcast_to(top_local, (8, KPAD))
    row = lax.broadcasted_iota(jnp.int32, (8, KPAD), 0)
    down = jnp.zeros((8, KPAD), F32)
    for child in range(8):
        down = jnp.where(row == child, dot3(dot_nn, top_rows, shift[child]), down)

    def gather(leaf, carry):
        base = leaf * 32
        expansions[pl.ds(leaf, 1), :] = tree(
            [table[pl.ds(far_index[base + e], 1), :] for e in range(32)]
        )
        return carry

    lax.fori_loop(0, LEAVES, gather, 0)
    return (expansions[...].reshape(8, 8, KPAD) + down[None]).reshape(LEAVES, KPAD)


def finish_kernel(
    count, codes, far_index, top_list, top_class,
    left, m2l, shift, own_moments, in_rows, near_own,
    harmonic_hbm, bodies_hbm, in_bodies_hbm,
    out,
    pool, harmonic, near, pool_moments, table, expansions, sems,
):
    slots = in_bodies_hbm.shape[0]
    copy_own = pltpu.make_async_copy(bodies_hbm, pool.at[pl.ds(0, LEAVES)], sems.at[0])
    copy_in = pltpu.make_async_copy(in_bodies_hbm, pool.at[pl.ds(LEAVES, slots)], sems.at[1])
    copy_harmonic = pltpu.make_async_copy(harmonic_hbm, harmonic, sems.at[2])
    copy_own.start()
    copy_in.start()
    copy_harmonic.start()
    near[...] = jnp.zeros_like(near)
    rows = LEAVES + slots
    pool_moments[:LEAVES] = own_moments[...]
    fine = in_rows.shape[1] // 3
    for peer in range(in_rows.shape[0]):
        start = LEAVES + 2 * fine * peer
        pool_moments[start : start + 2 * fine] = in_rows[peer, : 2 * fine]
    for e in range(32):
        owner = top_list[e]
        pool_moments[rows + e : rows + e + 1, :] = in_rows[
            owner // fine, pl.ds(2 * fine + lax.rem(owner, fine), 1), :
        ]
    local = local_expansions(pool_moments, m2l, shift, table, far_index, top_class, expansions)
    local_columns = jnp.concatenate([local, jnp.zeros((KPAD - LEAVES, KPAD), F32)], axis=0).T

    copy_own.wait()
    copy_in.wait()

    def near_step(group, carry):
        for member in range(UNROLL):
            code = codes[group * UNROLL + member]
            target = code & 63
            source = (code >> 6) & 1023
            live = (code >> 21).astype(F32)
            body = pad8(pool[source])
            right = source_right(body, (code >> 16) & 31)
            charge = body[3:4] * live
            for start in range(0, WIDTH, 128):
                near[target, start : start + 128] += pair_rows(
                    left.at[target][:, :GROUPS], right, charge, start, 128
                )
        return carry

    lax.fori_loop(0, (count[0] + UNROLL - 1) // UNROLL, near_step, 0)
    copy_harmonic.wait()
    ones = jnp.ones((8, 128), BF16)

    def far_step(group, columns):
        for member in range(8):
            leaf = group * 8 + member
            product = harmonic[leaf] * columns[:, member : member + 1]
            far = jnp.sum(product, axis=0, keepdims=True)
            near_high, near_low = split2(near[leaf])
            total = dot_nt(ones, near_high) + dot_nt(ones, near_low)
            out[pl.ds(leaf, 1), :] = total[:1] + far + near_own[pl.ds(leaf, 1), :]
        return pltpu.roll(columns, KPAD - 8, 1)

    lax.fori_loop(0, LEAVES // 8, far_step, local_columns)


def near_codes(near_src, near_shift, wanted):
    number = near_src.size
    flat = near_src.reshape(number)
    entry = jnp.arange(number, dtype=jnp.int32)
    code = (entry // near_src.shape[1]) + flat * 64 + near_shift.reshape(number) * 65536 + (1 << 21)
    wanted = wanted.reshape(number)
    place = jnp.sum(wanted[None, :] & (entry[None, :] < entry[:, None]), axis=1, dtype=jnp.int32)
    place = jnp.where(wanted, place, -1)
    codes = jnp.sum(jnp.where(place[None, :] == entry[:, None], code[None, :], 0), axis=1)
    return codes, jnp.sum(wanted, dtype=jnp.int32)[None]


SMEM = pl.BlockSpec(memory_space=pltpu.SMEM)
VMEM = pl.BlockSpec(memory_space=pltpu.VMEM)
ANY = pl.BlockSpec(memory_space=pl.ANY)


def pad_ops(ops):
    return jnp.pad(ops, ((0, 0), (0, KPAD - ops.shape[1]), (0, KPAD - ops.shape[2])))


def wave_rows(moment_freq, moment_phase):
    rows = jnp.concatenate([moment_freq, moment_phase[None] * (0.5 / math.pi)], axis=0)
    return jnp.pad(rows, ((0, 0), (0, KPAD - rows.shape[1])))


def run_finish(count, codes, far_index, top_list, top_class, left, m2l, shift, moments, in_rows, near_own, harmonic, bodies, in_bodies):
    slots = in_bodies.shape[0]
    rows = LEAVES + slots + 32
    return pl.pallas_call(
        finish_kernel,
        out_shape=jax.ShapeDtypeStruct((LEAVES, WIDTH), F32),
        in_specs=[SMEM] * 5 + [VMEM] * 6 + [ANY] * 3,
        out_specs=VMEM,
        scratch_shapes=[
            pltpu.VMEM((LEAVES + slots, 4, WIDTH), F32),
            pltpu.VMEM((LEAVES, KPAD, WIDTH), F32),
            pltpu.VMEM((LEAVES, WIDTH, 128), F32),
            pltpu.VMEM((rows, KPAD), F32),
            pltpu.VMEM((16 * rows + 8, KPAD), F32),
            pltpu.VMEM((LEAVES, KPAD), F32),
            pltpu.SemaphoreType.DMA((3,)),
        ],
        compiler_params=pltpu.CompilerParams(vmem_limit_bytes=62 << 20),
        cost_estimate=pl.CostEstimate(flops=60_000_000_000, bytes_accessed=40_000_000, transcendentals=0),
    )(count, codes, far_index, top_list, top_class, left, m2l, shift, moments, in_rows, near_own, harmonic, bodies, in_bodies)


def exchange_kernel(
    pairs, bodies, table, waves, shift,
    in_bodies, in_rows, harmonic_out, left_out, moments, near_own,
    r1, r2, r3, l1, l2, l3, opposite,
    packs, harmonic, left, transposed, column_rows, row_pack, tables, table_words,
    ring_send, ring_recv, small_send, small_recv, plane_send, plane_recv, local_sems, out_sems,
):
    gx, gy = lax.axis_index("gx"), lax.axis_index("gy")
    coarse, fine = row_pack.shape[0], column_rows.shape[0]
    right = {"gy": lax.rem(gy + 1, fine)}
    back = {"gy": lax.rem(gy + fine - 1, fine)}
    half = LEAVES // 2

    barrier = pltpu.get_barrier_semaphore()

    def greet_plane(j, carry):
        pl.semaphore_signal(barrier, inc=1, device_id={"gx": lax.rem(gx + j, coarse)})
        return carry

    lax.fori_loop(1, coarse, greet_plane, 0)
    for k in range(1, fine):
        pl.semaphore_signal(barrier, inc=1, device_id={"gy": lax.rem(gy + k, fine)})
    pl.semaphore_wait(barrier, coarse + fine - 2)

    def remote(source, target, send, recv, device):
        copy = pltpu.make_async_remote_copy(
            src_ref=source, dst_ref=target, send_sem=send, recv_sem=recv, device_id=device
        )
        copy.start()
        return copy

    def ring(step):
        if step == 4:
            return (
                remote(r3.at[pl.ds(0, half)], opposite.at[pl.ds(0, half)],
                       ring_send.at[6], ring_recv.at[6], right),
                remote(l3.at[pl.ds(half, half)], opposite.at[pl.ds(half, half)],
                       ring_send.at[7], ring_recv.at[7], back),
            )
        sources = ((bodies, bodies), (r1, l1), (r2, l2))[step - 1]
        targets = ((r1, l1), (r2, l2), (r3, l3))[step - 1]
        slot = 2 * (step - 1)
        return (
            remote(sources[0], targets[0], ring_send.at[slot], ring_recv.at[slot], right),
            remote(sources[1], targets[1], ring_send.at[slot + 1], ring_recv.at[slot + 1], back),
        )

    first = ring(1)
    for k in range(1, fine):
        there = lax.rem(gy + k, fine)
        remote(table.at[there], tables.at[k], small_send.at[0], small_recv.at[0], {"gy": there})
    own_table = pltpu.make_async_copy(table.at[gy], tables.at[0], local_sems.at[0])
    own_table.start()
    own_table.wait()
    others = tables.at[pl.ds(1, fine - 1)]
    pltpu.make_async_copy(others, others, small_recv.at[0]).wait()
    words = pltpu.make_async_copy(tables, table_words, local_sems.at[0])
    words.start()
    words.wait()

    def pack(block, offset):
        there = lax.rem(gy + fine - offset, fine)
        buffer = packs.at[offset]
        place = pl.ds((gx * fine + there) * 2, 2)

        def one(quad, carry):
            for part in range(4):
                peer = quad * 4 + part
                for slot in range(2):
                    buffer[peer, slot] = block[table_words[offset, 0, peer * 2 + slot]]
            return carry

        lax.fori_loop(0, coarse // 4, one, 0)

        def push(j, carry):
            peer = lax.rem(gx + j, coarse)
            remote(buffer.at[peer], in_bodies.at[place], plane_send.at[0], plane_recv.at[0],
                   {"gx": peer})
            return carry

        lax.fori_loop(1, coarse, push, 0)
        keep = pltpu.make_async_copy(buffer.at[gx], in_bodies.at[place], local_sems.at[1 + offset])
        keep.start()
        return keep

    kept = [pack(bodies, 0)]

    weights = phase_weights(waves[...])
    lane = lax.broadcasted_iota(jnp.int32, (KPAD, KPAD), 1)
    transposed[...] = jnp.zeros_like(transposed)

    def feature_step(pair, carry):
        for member in range(2):
            leaf = pair * 2 + member
            body = pad8(bodies[leaf])
            basis = basis_leaf(body, weights)
            harmonic[leaf] = basis
            column = jnp.sum(lane_fold(basis * body[3:4]), axis=1, keepdims=True)
            transposed[...] = jnp.where(lane == leaf, column, transposed[...])
            left[leaf, :, :GROUPS] = left_side(body).T.astype(BF16)
        return carry

    def near_step(pair, carry):
        for member in range(4):
            leaf = pair * 4 + member
            sides = []
            for entry in range(2):
                code = pairs[leaf * 2 + entry]
                body = pad8(bodies[code & 63])
                charge = body[3:4] * (code >> 21).astype(F32)
                sides.append((source_right(body, (code >> 16) & 31), charge))
            rows = left[leaf][:, :GROUPS]
            pieces = []
            for start in range(0, WIDTH, 128):
                total = sum(pair_rows(rows, side, charge, start, 128) for side, charge in sides)
                high, low = split2(total)
                pieces.append(dot_nt(ones, high) + dot_nt(ones, low))
            near_own[pl.ds(leaf, 1), :] = jnp.concatenate(pieces, axis=1)[:1]
        return carry

    ones = jnp.ones((8, 128), BF16)
    left[...] = jnp.zeros_like(left)
    cuts = (0, 24, 48, 64)
    lax.fori_loop(cuts[0] // 2, cuts[1] // 2, feature_step, 0)

    first[0].wait_recv()
    first[1].wait_recv()
    second = ring(2)
    kept += [pack(r1, 1), pack(l1, fine - 1)]
    lax.fori_loop(cuts[1] // 2, cuts[2] // 2, feature_step, 0)

    second[0].wait_recv()
    second[1].wait_recv()
    third = ring(3)
    kept += [pack(r2, 2), pack(l2, fine - 2)]
    lax.fori_loop(cuts[2] // 2, cuts[3] // 2, feature_step, 0)

    outs = [
        pltpu.make_async_copy(harmonic, harmonic_out, out_sems.at[0]),
        pltpu.make_async_copy(left, left_out, out_sems.at[1]),
    ]
    for copy in outs:
        copy.start()
    own = transposed[...].T[:LEAVES]
    moments[...] = own
    column_rows[0, :LEAVES] = own
    column_rows[0, LEAVES:] = jnp.broadcast_to(upward(own, shift), (8, KPAD))
    for k in range(1, fine):
        remote(column_rows.at[0], column_rows.at[k], small_send.at[1], small_recv.at[1],
               {"gy": lax.rem(gy + k, fine)})

    third[0].wait_recv()
    third[1].wait_recv()
    fourth = ring(4)
    kept += [pack(r3, 3), pack(l3, fine - 3)]
    lax.fori_loop(0, half // 4, near_step, 0)

    fourth[0].wait_recv()
    fourth[1].wait_recv()
    kept += [pack(opposite, fine // 2)]

    others = column_rows.at[pl.ds(1, fine - 1)]
    pltpu.make_async_copy(others, others, small_recv.at[1]).wait()
    for offset in range(fine):
        there = lax.rem(gy + fine - offset, fine)

        def pick(peer, carry):
            for slot in range(2):
                row = table_words[offset, 0, peer * 2 + slot]
                row_pack[peer, pl.ds(there * 2 + slot, 1), :] = column_rows[offset, pl.ds(row, 1), :]
            row_pack[peer, pl.ds(2 * fine + there, 1), :] = column_rows[offset, LEAVES : LEAVES + 1, :]
            return carry

        lax.fori_loop(0, coarse, pick, 0)

    def push_rows(j, carry):
        peer = lax.rem(gx + j, coarse)
        remote(row_pack.at[peer], in_rows.at[gx], plane_send.at[1], plane_recv.at[1], {"gx": peer})
        return carry

    lax.fori_loop(1, coarse, push_rows, 0)
    keep = pltpu.make_async_copy(row_pack.at[gx], in_rows.at[gx], local_sems.at[0])
    keep.start()
    kept.append(keep)

    lax.fori_loop(half // 4, LEAVES // 4, near_step, 0)

    for copy in kept + outs:
        copy.wait()
    for copy in first + second + third + fourth:
        copy.wait_send()
    sent_tables = tables.at[pl.ds(1, fine - 1)]
    pltpu.make_async_copy(sent_tables, sent_tables, small_send.at[0]).wait()
    pltpu.make_async_copy(others, others, small_send.at[1]).wait()
    sent = in_bodies.at[pl.ds(0, (coarse - 1) * fine * 2)]
    pltpu.make_async_copy(sent, sent, plane_send.at[0]).wait()
    pltpu.make_async_copy(sent, sent, plane_recv.at[0]).wait()
    sent = in_rows.at[pl.ds(0, coarse - 1)]
    pltpu.make_async_copy(sent, sent, plane_send.at[1]).wait()
    pltpu.make_async_copy(sent, sent, plane_recv.at[1]).wait()


def run_exchange(pairs, bodies, table, waves, shift, coarse, fine):
    block = pltpu.VMEM((LEAVES, 4, WIDTH), F32)
    return pl.pallas_call(
        exchange_kernel,
        out_shape=[
            jax.ShapeDtypeStruct((coarse * fine * 2, 4, WIDTH), F32),
            jax.ShapeDtypeStruct((coarse, 3 * fine, KPAD), F32),
            jax.ShapeDtypeStruct((LEAVES, KPAD, WIDTH), F32),
            jax.ShapeDtypeStruct((LEAVES, WIDTH, 128), BF16),
            jax.ShapeDtypeStruct((LEAVES, KPAD), F32),
            jax.ShapeDtypeStruct((LEAVES, WIDTH), F32),
        ],
        in_specs=[SMEM] + [VMEM] * 4,
        out_specs=[ANY] * 4 + [VMEM] * 2,
        scratch_shapes=[block] * 7
        + [
            pltpu.VMEM((fine, coarse, 2, 4, WIDTH), F32),
            pltpu.VMEM((LEAVES, KPAD, WIDTH), F32),
            pltpu.VMEM((LEAVES, WIDTH, 128), BF16),
            pltpu.VMEM((KPAD, KPAD), F32),
            pltpu.VMEM((fine, LEAVES + 8, KPAD), F32),
            pltpu.VMEM((coarse, 3 * fine, KPAD), F32),
            pltpu.VMEM((fine, 8, 128), jnp.int32),
            pltpu.SMEM((fine, 8, 128), jnp.int32),
            pltpu.SemaphoreType.DMA((8,)),
            pltpu.SemaphoreType.DMA((8,)),
            pltpu.SemaphoreType.DMA((2,)),
            pltpu.SemaphoreType.DMA((2,)),
            pltpu.SemaphoreType.DMA((2,)),
            pltpu.SemaphoreType.DMA((2,)),
            pltpu.SemaphoreType.DMA((1 + fine,)),
            pltpu.SemaphoreType.DMA((2,)),
        ],
        compiler_params=pltpu.CompilerParams(
            vmem_limit_bytes=60 << 20, collective_id=0, has_side_effects=True
        ),
        cost_estimate=pl.CostEstimate(flops=40_000_000_000, bytes_accessed=40_000_000, transcendentals=0),
    )(pairs, bodies, table, waves, shift)


def local(
    positions,
    charges,
    moment_freq,
    moment_phase,
    m2l_ops,
    child_parent_shift_matrix,
    send_leaf,
    send_count,
    far_src,
    far_class,
    near_src,
    near_shift,
    top_list,
    top_class,
):
    leaves = far_src.shape[0]
    peers, slot_count = send_leaf.shape[1:]
    coarse = lax.axis_size("gx")
    fine = lax.axis_size("gy")
    bodies = (
        jnp.concatenate([positions, charges[None, :]], axis=0)
        .reshape(4, leaves, WIDTH)
        .transpose(1, 0, 2)
    )
    table = send_leaf[0].reshape(coarse, fine, slot_count).transpose(1, 0, 2)
    table = jnp.pad(
        table.reshape(fine, 1, coarse * slot_count),
        ((0, 0), (0, 7), (0, 128 - coarse * slot_count)),
    )
    column = jnp.arange(near_src.shape[1], dtype=jnp.int32)[None, :]
    own = (near_src >= 0) & (near_src < leaves) & (column > 0)
    first_own = jnp.min(jnp.where(own, column, near_src.shape[1]), axis=1, keepdims=True)
    taken = column == first_own
    word = near_src + near_shift * 65536 + (1 << 21)
    pairs = jnp.stack(
        [word[:, 0], jnp.sum(jnp.where(taken, word, 0), axis=1)], axis=1
    ).reshape(-1)
    waves = wave_rows(moment_freq, moment_phase)
    shift = pad_ops(child_parent_shift_matrix)
    in_bodies, in_rows, harmonic, left, moments, near_own = run_exchange(
        pairs, bodies, table, waves, shift, coarse, fine
    )
    wanted = (near_src >= 0) & (column > 0) & ~taken
    codes, count = near_codes(near_src, near_shift, wanted)
    rows = leaves + peers * slot_count + 32
    far_index = jnp.where(far_src >= 0, far_class * rows + far_src, 16 * rows).reshape(-1)
    result = run_finish(
        count, codes, far_index, top_list[0], top_class[0], left, pad_ops(m2l_ops), shift,
        moments, in_rows, near_own, harmonic, bodies, in_bodies,
    )
    return result.reshape(leaves * WIDTH)


def solution(mesh):
    placed = (
        P(None, ("gx", "gy")),
        P(("gx", "gy")),
        P(),
        P(),
        P(),
        P(),
        P(("gx", "gy"), None, None),
        P(("gx", "gy"), None),
        P(("gx", "gy"), None),
        P(("gx", "gy"), None),
        P(("gx", "gy"), None),
        P(("gx", "gy"), None),
        P(("gx", "gy"), None),
        P(("gx", "gy"), None),
    )
    return jax.shard_map(
        local, mesh=mesh, in_specs=placed, out_specs=P(("gx", "gy")), check_vma=False
    )
```

```python
import functools
import math

import jax
import jax.numpy as jnp
from jax import lax
from jax.experimental import pallas as pl
from jax.experimental.pallas import tpu as pltpu
from jax.sharding import PartitionSpec as P

F32 = jnp.float32
BF16 = jnp.bfloat16
SOFTENING = 0.01
LEAVES = 64
WIDTH = 512
KPAD = 128
GROUPS = 48
UNROLL = 8
COS = (1.0, -19.73920440673828, 64.93911743164062, -85.45011138916016, 60.16743087768555, -25.96688461303711, 6.527706146240234)


def split2(a):
    high = a.astype(BF16)
    return high, (a - high.astype(F32)).astype(BF16)


def split3(a):
    high = a.astype(BF16).astype(F32)
    rest = a - high
    middle = rest.astype(BF16).astype(F32)
    return high, middle, rest - middle


def dot_nt(a, b):
    return lax.dot_general(a, b, (((1,), (1,)), ((), ())), preferred_element_type=F32)


def dot_nn(a, b):
    return jnp.dot(a, b, preferred_element_type=F32)


def dot3(dot, a, b):
    a_high, a_low = split2(a)
    b_high, b_low = split2(b)
    return dot(a_high, b_high) + (dot(a_high, b_low) + dot(a_low, b_high))


def pad8(record):
    return jnp.concatenate([record, jnp.zeros((4, record.shape[1]), F32)], axis=0)


def right_side(body, centre):
    row = lax.broadcasted_iota(jnp.int32, body.shape, 0)
    point = jnp.where(row < 3, body - centre, 0.0)
    norm = jnp.sum(point * point, axis=0, keepdims=True) + SOFTENING
    high, middle, low = split3(jnp.where(row == 3, norm, -2.0 * point))
    high_one = jnp.where(row == 3, 1.0, high)
    middle_one = jnp.where(row == 3, 1.0, middle)
    return jnp.concatenate([high, middle, high_one, low, high_one, middle_one], axis=0).astype(BF16)


def left_side(body):
    row = lax.broadcasted_iota(jnp.int32, body.shape, 0)
    point = jnp.where(row < 3, body - 0.5, 0.0)
    norm = jnp.sum(point * point, axis=0, keepdims=True)
    high, middle, low = split3(jnp.where(row == 3, norm, point))
    one = jnp.where(row == 3, 1.0, high)
    return jnp.concatenate(
        [
            one,
            one,
            jnp.where(row == 3, high, middle),
            one,
            jnp.where(row == 3, middle, low),
            jnp.where(row == 3, low, middle),
        ],
        axis=0,
    )


def phase_weights(waves):
    waves = pad8(waves)
    row = lax.broadcasted_iota(jnp.int32, waves.shape, 0)
    freq = jnp.where(row < 3, waves, 0.0)
    turn = jnp.sum(jnp.where(row < 3, 0.5 * waves, waves), axis=0, keepdims=True)
    turn = turn - jnp.round(turn)
    high, middle, low = split3(jnp.where(row == 3, turn, -0.5 * freq))
    plain = jnp.where(row == 3, 0.0, high)
    groups = jnp.concatenate(
        [
            plain,
            plain,
            jnp.where(row == 3, high, middle),
            plain,
            jnp.where(row == 3, middle, low),
            jnp.where(row == 3, low, middle),
        ],
        axis=0,
    )
    return groups.T.astype(BF16)


def cosine_turns(turns):
    rest = turns - jnp.round(turns)
    square = rest * rest
    value = jnp.full_like(square, COS[-1])
    for coefficient in COS[-2::-1]:
        value = value * square + coefficient
    return value


def lane_fold(a):
    return (a[:, :128] + a[:, 128:256]) + (a[:, 256:384] + a[:, 384:])


def basis_leaf(body, weights):
    return cosine_turns(dot_nn(weights, right_side(body, 0.5)))


def upward(moments, shift_ref):
    grouped = moments.reshape(8, 8, KPAD).sum(axis=0)
    row = lax.broadcasted_iota(jnp.int32, grouped.shape, 0)
    total = jnp.zeros((8, KPAD), F32)
    for child in range(8):
        total = total + dot3(dot_nt, jnp.where(row == child, grouped, 0.0), shift_ref[child])
    return jnp.sum(total, axis=0, keepdims=True)


def offset_vector(code):
    return (
        (code % 3 - 1).astype(F32),
        (code // 3 % 3 - 1).astype(F32),
        (code // 9 - 1).astype(F32),
    )


def source_right(body, shift):
    row = lax.broadcasted_iota(jnp.int32, body.shape, 0)
    shift_x, shift_y, shift_z = offset_vector(shift)
    centre = 0.5 - jnp.where(row == 0, shift_x, jnp.where(row == 1, shift_y, shift_z))
    return right_side(body, centre)


def pair_rows(left, right, charge, start, size):
    value = charge * lax.rsqrt(dot_nn(left[start : start + size], right))
    return lane_fold(value)


def near_fields(near_src, near_shift):
    source = near_src[...]
    column = lax.broadcasted_iota(jnp.int32, source.shape, 0)
    own = (source >= 0) & (source < LEAVES) & (column > 0)
    first_own = jnp.min(jnp.where(own, column.astype(F32), 8.0), axis=0, keepdims=True)
    taken = column.astype(F32) == first_own
    wanted = (source >= 0) & (column > 0) & jnp.logical_not(taken)
    word = (source + near_shift[...] * 65536 + (1 << 21)).astype(F32)
    return word, taken, wanted, source


def near_list(near_src, near_shift, listed):
    word, _, wanted, source = near_fields(near_src, near_shift)
    word = word + (source * 63 + lax.broadcasted_iota(jnp.int32, source.shape, 1)).astype(F32)
    mark = jnp.where(wanted, 1.0, 0.0)
    before = lax.broadcasted_iota(jnp.int32, (LEAVES, LEAVES), 0)
    before = before < lax.broadcasted_iota(jnp.int32, (LEAVES, LEAVES), 1)
    place = dot_nn(mark.astype(BF16), jnp.where(before, 1.0, 0.0).astype(BF16))
    totals = jnp.sum(mark, axis=1, keepdims=True)
    row = lax.broadcasted_iota(jnp.int32, (8, LEAVES), 0)
    for column in range(8):
        place = place + jnp.where(row > column, totals[column : column + 1], 0.0)
    place = jnp.where(wanted, place, -1.0).astype(jnp.int32)
    parts = split3(word)
    low_row = lax.broadcasted_iota(jnp.int32, (LEAVES, LEAVES), 0)
    codes = jnp.zeros((8, LEAVES), F32)
    for column in range(8):
        at = place[column : column + 1]
        low = jnp.where(low_row == (at & 63), 1.0, 0.0).astype(BF16)
        for part in parts:
            high = jnp.where(row == (at >> 6), part[column : column + 1], 0.0).astype(BF16)
            codes = codes + dot_nt(high, low)
    number = jnp.broadcast_to(jnp.sum(totals, axis=0, keepdims=True), (8, 128))
    listed[...] = number.astype(jnp.int32)
    listed[:, :LEAVES] = codes.astype(jnp.int32)


def pad_into(padded, ops):
    padded[...] = jnp.zeros_like(padded)
    padded[:, : ops.shape[1], : ops.shape[2]] = ops[...]


def local_expansions(pool_moments, m2l, shift, table, far_index, top_class, expansions):
    rows = pool_moments.shape[0]
    pool_high, pool_low = split2(pool_moments[...])
    for pair in range(8):
        op_high, op_low = split2(m2l[2 * pair : 2 * pair + 2].reshape(256, KPAD))
        moved = dot_nt(pool_high, op_high) + (dot_nt(pool_high, op_low) + dot_nt(pool_low, op_high))
        table[2 * pair * rows : (2 * pair + 1) * rows] = moved[:, :KPAD]
        table[(2 * pair + 1) * rows : (2 * pair + 2) * rows] = moved[:, KPAD:]
    table[16 * rows : 16 * rows + 8] = jnp.zeros((8, KPAD), F32)

    def tree(parts):
        while len(parts) > 1:
            parts = [a + b for a, b in zip(parts[::2], parts[1::2])]
        return parts[0]

    top_local = tree(
        [table[pl.ds(top_class[0, e] * rows + (rows - 32 + e), 1), :] for e in range(32)]
    )
    top_rows = jnp.broadcast_to(top_local, (8, KPAD))
    row = lax.broadcasted_iota(jnp.int32, (8, KPAD), 0)
    down = jnp.zeros((8, KPAD), F32)
    for child in range(8):
        down = jnp.where(row == child, dot3(dot_nn, top_rows, shift[child]), down)

    def gather(leaf, carry):
        expansions[pl.ds(leaf, 1), :] = tree(
            [table[pl.ds(far_index[e, leaf], 1), :] for e in range(32)]
        )
        return carry

    lax.fori_loop(0, LEAVES, gather, 0)
    return (expansions[...].reshape(8, 8, KPAD) + down[None]).reshape(LEAVES, KPAD)


def finish_kernel(
    top_list, top_class,
    near_src, near_shift, far_src, far_class, m2l_ops, shift_ops, own_moments, in_rows,
    left_hbm, near_hbm, harmonic_hbm, bodies_hbm, in_bodies_hbm,
    out,
    pool, left, near, harmonic, pool_moments, table, expansions, m2l, shift,
    listed, far_rows, codes, far_index, sems,
):
    slots = in_bodies_hbm.shape[0]
    copies = [
        pltpu.make_async_copy(source, target, sems.at[place])
        for place, (source, target) in enumerate(
            (
                (left_hbm, left),
                (bodies_hbm, pool.at[pl.ds(0, LEAVES)]),
                (in_bodies_hbm, pool.at[pl.ds(LEAVES, slots)]),
                (near_hbm, near),
                (harmonic_hbm, harmonic),
            )
        )
    ]
    for copy in copies:
        copy.start()
    entry_rows = 16 * (LEAVES + slots + 32)
    source = far_src[...]
    far_rows[...] = jnp.zeros_like(far_rows)
    far_rows[:, :LEAVES] = jnp.where(
        source >= 0, far_class[...] * (entry_rows // 16) + source, entry_rows
    )
    near_list(near_src, near_shift, listed)
    words = [
        pltpu.make_async_copy(far_rows, far_index, sems.at[5]),
        pltpu.make_async_copy(listed, codes, sems.at[6]),
    ]
    for copy in words:
        copy.start()
    pad_into(m2l, m2l_ops)
    pad_into(shift, shift_ops)
    rows = LEAVES + slots
    pool_moments[:LEAVES] = own_moments[...]
    fine = in_rows.shape[1] // 3
    for peer in range(in_rows.shape[0]):
        start = LEAVES + 2 * fine * peer
        pool_moments[start : start + 2 * fine] = in_rows[peer, : 2 * fine]
    for e in range(32):
        owner = top_list[0, e]
        pool_moments[rows + e : rows + e + 1, :] = in_rows[
            owner // fine, pl.ds(2 * fine + lax.rem(owner, fine), 1), :
        ]
    for copy in words:
        copy.wait()
    local = local_expansions(pool_moments, m2l, shift, table, far_index, top_class, expansions)
    local_columns = jnp.concatenate([local, jnp.zeros((KPAD - LEAVES, KPAD), F32)], axis=0).T

    for copy in copies[:4]:
        copy.wait()

    def near_step(group, carry):
        for member in range(UNROLL):
            code = codes[group >> 3, (group & 7) * UNROLL + member]
            target = code & 63
            source = (code >> 6) & 1023
            live = (code >> 21).astype(F32)
            body = pad8(pool[source])
            right = source_right(body, (code >> 16) & 31)
            charge = body[3:4] * live
            for start in range(0, WIDTH, 128):
                near[target, start : start + 128] += pair_rows(
                    left.at[target][:, :GROUPS], right, charge, start, 128
                )
        return carry

    lax.fori_loop(0, (codes[0, LEAVES] + UNROLL - 1) // UNROLL, near_step, 0)
    copies[4].wait()
    ones = jnp.ones((8, 128), BF16)

    def far_step(group, columns):
        for member in range(8):
            leaf = group * 8 + member
            product = harmonic[leaf] * columns[:, member : member + 1]
            far = jnp.sum(product, axis=0, keepdims=True)
            near_high, near_low = split2(near[leaf])
            total = dot_nt(ones, near_high) + dot_nt(ones, near_low)
            out[leaf] = total[:1] + far
        return pltpu.roll(columns, KPAD - 8, 1)

    lax.fori_loop(0, LEAVES // 8, far_step, local_columns)


SMEM = pl.BlockSpec(memory_space=pltpu.SMEM)
VMEM = pl.BlockSpec(memory_space=pltpu.VMEM)
ANY = pl.BlockSpec(memory_space=pl.ANY)


def run_finish(
    top_list, top_class, near_src, near_shift, far_src, far_class, m2l, shift, moments, in_rows,
    left, near, harmonic, bodies, in_bodies,
):
    slots = in_bodies.shape[0]
    rows = LEAVES + slots + 32
    return pl.pallas_call(
        finish_kernel,
        out_shape=jax.ShapeDtypeStruct((LEAVES, 1, WIDTH), F32),
        in_specs=[SMEM] * 2 + [VMEM] * 8 + [ANY] * 5,
        out_specs=VMEM,
        scratch_shapes=[
            pltpu.VMEM((LEAVES + slots, 4, WIDTH), F32),
            pltpu.VMEM((LEAVES, WIDTH, 128), BF16),
            pltpu.VMEM((LEAVES, WIDTH, 128), F32),
            pltpu.VMEM((LEAVES, KPAD, WIDTH), F32),
            pltpu.VMEM((rows, KPAD), F32),
            pltpu.VMEM((16 * rows + 8, KPAD), F32),
            pltpu.VMEM((LEAVES, KPAD), F32),
            pltpu.VMEM((16, KPAD, KPAD), F32),
            pltpu.VMEM((8, KPAD, KPAD), F32),
            pltpu.VMEM((8, 128), jnp.int32),
            pltpu.VMEM((32, 128), jnp.int32),
            pltpu.SMEM((8, 128), jnp.int32),
            pltpu.SMEM((32, 128), jnp.int32),
            pltpu.SemaphoreType.DMA((7,)),
        ],
        compiler_params=pltpu.CompilerParams(vmem_limit_bytes=62 << 20),
        cost_estimate=pl.CostEstimate(flops=60_000_000_000, bytes_accessed=40_000_000, transcendentals=0),
    )(
        top_list, top_class, near_src, near_shift, far_src, far_class, m2l, shift, moments, in_rows,
        left, near, harmonic, bodies, in_bodies,
    )


def exchange_kernel(
    positions, charges, send_table, near_src, near_shift, freq, phase, shift_ops,
    in_bodies, in_rows, harmonic_out, left_out, near_out, moments, bodies,
    r1, r2, r3, l1, l2, l3, opposite,
    packs, harmonic, left, near, shift, waves, transposed, column_rows, row_pack,
    table, tables, table_words, pair_words, pairs,
    ring_send, ring_recv, small_send, small_recv, plane_send, plane_recv, local_sems, out_sems,
):
    gx, gy = lax.axis_index("gx"), lax.axis_index("gy")
    coarse, fine = row_pack.shape[0], column_rows.shape[0]
    right = {"gy": lax.rem(gy + 1, fine)}
    back = {"gy": lax.rem(gy + fine - 1, fine)}
    half = LEAVES // 2

    def build(quad, carry):
        for member in range(4):
            leaf = quad * 4 + member
            place = pl.ds(pl.multiple_of(leaf * WIDTH, WIDTH), WIDTH)
            bodies[leaf] = jnp.concatenate([positions[:, place], charges[leaf]], axis=0)
        return carry

    lax.fori_loop(0, LEAVES // 4, build, 0)
    table[...] = jnp.zeros_like(table)
    table[: send_table.shape[0], :] = send_table[...]
    barrier = pltpu.get_barrier_semaphore()

    def greet_plane(j, carry):
        pl.semaphore_signal(barrier, inc=1, device_id={"gx": lax.rem(gx + j, coarse)})
        return carry

    lax.fori_loop(1, coarse, greet_plane, 0)
    for k in range(1, fine):
        pl.semaphore_signal(barrier, inc=1, device_id={"gy": lax.rem(gy + k, fine)})
    pl.semaphore_wait(barrier, coarse + fine - 2)

    def remote(source, target, send, recv, device):
        copy = pltpu.make_async_remote_copy(
            src_ref=source, dst_ref=target, send_sem=send, recv_sem=recv, device_id=device
        )
        copy.start()
        return copy

    def ring(step):
        if step == 4:
            return (
                remote(r3.at[pl.ds(0, half)], opposite.at[pl.ds(0, half)],
                       ring_send.at[6], ring_recv.at[6], right),
                remote(l3.at[pl.ds(half, half)], opposite.at[pl.ds(half, half)],
                       ring_send.at[7], ring_recv.at[7], back),
            )
        sources = ((bodies, bodies), (r1, l1), (r2, l2))[step - 1]
        targets = ((r1, l1), (r2, l2), (r3, l3))[step - 1]
        slot = 2 * (step - 1)
        return (
            remote(sources[0], targets[0], ring_send.at[slot], ring_recv.at[slot], right),
            remote(sources[1], targets[1], ring_send.at[slot + 1], ring_recv.at[slot + 1], back),
        )

    first = ring(1)
    for k in range(1, fine):
        there = lax.rem(gy + k, fine)
        remote(table, tables.at[k], small_send.at[0], small_recv.at[0], {"gy": there})
    own_table = pltpu.make_async_copy(table, tables.at[0], local_sems.at[0])
    own_table.start()
    own_table.wait()
    others = tables.at[pl.ds(1, fine - 1)]
    pltpu.make_async_copy(others, others, small_recv.at[0]).wait()
    words = pltpu.make_async_copy(tables, table_words, local_sems.at[0])
    words.start()
    words.wait()

    def pack(block, offset):
        there = lax.rem(gy + fine - offset, fine)
        buffer = packs.at[offset]
        place = pl.ds((gx * fine + there) * 2, 2)

        def one(quad, carry):
            for part in range(4):
                peer = quad * 4 + part
                for slot in range(2):
                    buffer[peer, slot] = block[table_words[offset, slot, peer * fine + gy]]
            return carry

        lax.fori_loop(0, coarse // 4, one, 0)

        def push(j, carry):
            peer = lax.rem(gx + j, coarse)
            remote(buffer.at[peer], in_bodies.at[place], plane_send.at[0], plane_recv.at[0],
                   {"gx": peer})
            return carry

        lax.fori_loop(1, coarse, push, 0)
        keep = pltpu.make_async_copy(buffer.at[gx], in_bodies.at[place], local_sems.at[1 + offset])
        keep.start()
        return keep

    kept = [pack(bodies, 0)]

    word, taken, _, _ = near_fields(near_src, near_shift)
    pair_words[...] = jnp.zeros_like(pair_words)
    pair_words[:1, :LEAVES] = word[:1].astype(jnp.int32)
    pair_words[1:2, :LEAVES] = jnp.sum(
        jnp.where(taken, word, 0.0), axis=0, keepdims=True
    ).astype(jnp.int32)
    words = pltpu.make_async_copy(pair_words, pairs, local_sems.at[0])
    words.start()
    words.wait()
    pad_into(shift, shift_ops)
    waves[...] = jnp.zeros_like(waves)
    waves[:3, : freq.shape[1]] = freq[...]
    waves[3:4, : freq.shape[1]] = phase[...] * (0.5 / math.pi)
    weights = phase_weights(waves[...])
    lane = lax.broadcasted_iota(jnp.int32, (KPAD, KPAD), 1)
    transposed[...] = jnp.zeros_like(transposed)

    def feature_step(quad, carry):
        for member in range(4):
            leaf = quad * 4 + member
            body = pad8(bodies[leaf])
            basis = basis_leaf(body, weights)
            harmonic[leaf] = basis
            column = jnp.sum(lane_fold(basis * body[3:4]), axis=1, keepdims=True)
            transposed[...] = jnp.where(lane == leaf, column, transposed[...])
            left[leaf, :, :GROUPS] = left_side(body).T.astype(BF16)
        return carry

    def near_step(quad, carry):
        for member in range(4):
            leaf = quad * 4 + member
            sides = []
            for entry in range(2):
                code = pairs[entry, leaf]
                body = pad8(bodies[code & 63])
                charge = body[3:4] * (code >> 21).astype(F32)
                sides.append((source_right(body, (code >> 16) & 31), charge))
            rows = left[leaf][:, :GROUPS]
            for start in range(0, WIDTH, 128):
                near[leaf, start : start + 128] = sum(
                    pair_rows(rows, side, charge, start, 128) for side, charge in sides
                )
        return carry

    left[...] = jnp.zeros_like(left)
    cuts = (0, 24, 48, 64)
    lax.fori_loop(cuts[0] // 4, cuts[1] // 4, feature_step, 0)

    first[0].wait_recv()
    first[1].wait_recv()
    second = ring(2)
    kept += [pack(r1, 1), pack(l1, fine - 1)]
    lax.fori_loop(cuts[1] // 4, cuts[2] // 4, feature_step, 0)

    second[0].wait_recv()
    second[1].wait_recv()
    third = ring(3)
    kept += [pack(r2, 2), pack(l2, fine - 2)]
    lax.fori_loop(cuts[2] // 4, cuts[3] // 4, feature_step, 0)

    outs = [
        pltpu.make_async_copy(harmonic, harmonic_out, out_sems.at[0]),
        pltpu.make_async_copy(left, left_out, out_sems.at[1]),
    ]
    for copy in outs:
        copy.start()
    own = transposed[...].T[:LEAVES]
    moments[...] = own
    column_rows[0, :LEAVES] = own
    column_rows[0, LEAVES:] = jnp.broadcast_to(upward(own, shift), (8, KPAD))
    for k in range(1, fine):
        remote(column_rows.at[0], column_rows.at[k], small_send.at[1], small_recv.at[1],
               {"gy": lax.rem(gy + k, fine)})

    third[0].wait_recv()
    third[1].wait_recv()
    fourth = ring(4)
    kept += [pack(r3, 3), pack(l3, fine - 3)]
    lax.fori_loop(0, half // 4, near_step, 0)
    outs.append(
        pltpu.make_async_copy(near.at[pl.ds(0, half)], near_out.at[pl.ds(0, half)], out_sems.at[2])
    )
    outs[-1].start()

    fourth[0].wait_recv()
    fourth[1].wait_recv()
    kept += [pack(opposite, fine // 2)]

    others = column_rows.at[pl.ds(1, fine - 1)]
    pltpu.make_async_copy(others, others, small_recv.at[1]).wait()
    for offset in range(fine):
        there = lax.rem(gy + fine - offset, fine)

        def pick(quad, carry):
            for part in range(4):
                peer = quad * 4 + part
                for slot in range(2):
                    row = table_words[offset, slot, peer * fine + gy]
                    row_pack[peer, pl.ds(there * 2 + slot, 1), :] = column_rows[
                        offset, pl.ds(row, 1), :
                    ]
                row_pack[peer, pl.ds(2 * fine + there, 1), :] = column_rows[
                    offset, LEAVES : LEAVES + 1, :
                ]
            return carry

        lax.fori_loop(0, coarse // 4, pick, 0)

    def push_rows(j, carry):
        peer = lax.rem(gx + j, coarse)
        remote(row_pack.at[peer], in_rows.at[gx], plane_send.at[1], plane_recv.at[1], {"gx": peer})
        return carry

    lax.fori_loop(1, coarse, push_rows, 0)
    keep = pltpu.make_async_copy(row_pack.at[gx], in_rows.at[gx], local_sems.at[0])
    keep.start()
    kept.append(keep)

    lax.fori_loop(half // 4, LEAVES // 4, near_step, 0)
    outs.append(
        pltpu.make_async_copy(
            near.at[pl.ds(half, half)], near_out.at[pl.ds(half, half)], out_sems.at[3]
        )
    )
    outs[-1].start()

    for copy in kept + outs:
        copy.wait()
    for copy in first + second + third + fourth:
        copy.wait_send()
    sent_tables = tables.at[pl.ds(1, fine - 1)]
    pltpu.make_async_copy(sent_tables, sent_tables, small_send.at[0]).wait()
    pltpu.make_async_copy(others, others, small_send.at[1]).wait()
    sent = in_bodies.at[pl.ds(0, (coarse - 1) * fine * 2)]
    pltpu.make_async_copy(sent, sent, plane_send.at[0]).wait()
    pltpu.make_async_copy(sent, sent, plane_recv.at[0]).wait()
    sent = in_rows.at[pl.ds(0, coarse - 1)]
    pltpu.make_async_copy(sent, sent, plane_send.at[1]).wait()
    pltpu.make_async_copy(sent, sent, plane_recv.at[1]).wait()


def run_exchange(positions, charges, send_table, near_src, near_shift, freq, phase, shift, coarse, fine):
    block = pltpu.VMEM((LEAVES, 4, WIDTH), F32)
    return pl.pallas_call(
        exchange_kernel,
        out_shape=[
            jax.ShapeDtypeStruct((coarse * fine * 2, 4, WIDTH), F32),
            jax.ShapeDtypeStruct((coarse, 3 * fine, KPAD), F32),
            jax.ShapeDtypeStruct((LEAVES, KPAD, WIDTH), F32),
            jax.ShapeDtypeStruct((LEAVES, WIDTH, 128), BF16),
            jax.ShapeDtypeStruct((LEAVES, WIDTH, 128), F32),
            jax.ShapeDtypeStruct((LEAVES, KPAD), F32),
            jax.ShapeDtypeStruct((LEAVES, 4, WIDTH), F32),
        ],
        in_specs=[VMEM] * 8,
        out_specs=[ANY] * 5 + [VMEM] * 2,
        scratch_shapes=[block] * 7
        + [
            pltpu.VMEM((fine, coarse, 2, 4, WIDTH), F32),
            pltpu.VMEM((LEAVES, KPAD, WIDTH), F32),
            pltpu.VMEM((LEAVES, WIDTH, 128), BF16),
            pltpu.VMEM((LEAVES, WIDTH, 128), F32),
            pltpu.VMEM((8, KPAD, KPAD), F32),
            pltpu.VMEM((4, KPAD), F32),
            pltpu.VMEM((KPAD, KPAD), F32),
            pltpu.VMEM((fine, LEAVES + 8, KPAD), F32),
            pltpu.VMEM((coarse, 3 * fine, KPAD), F32),
            pltpu.VMEM((8, coarse * fine), jnp.int32),
            pltpu.VMEM((fine, 8, coarse * fine), jnp.int32),
            pltpu.SMEM((fine, 8, coarse * fine), jnp.int32),
            pltpu.VMEM((8, 128), jnp.int32),
            pltpu.SMEM((8, 128), jnp.int32),
            pltpu.SemaphoreType.DMA((8,)),
            pltpu.SemaphoreType.DMA((8,)),
            pltpu.SemaphoreType.DMA((2,)),
            pltpu.SemaphoreType.DMA((2,)),
            pltpu.SemaphoreType.DMA((2,)),
            pltpu.SemaphoreType.DMA((2,)),
            pltpu.SemaphoreType.DMA((1 + fine,)),
            pltpu.SemaphoreType.DMA((4,)),
        ],
        compiler_params=pltpu.CompilerParams(
            vmem_limit_bytes=62 << 20, collective_id=0, has_side_effects=True
        ),
        cost_estimate=pl.CostEstimate(flops=40_000_000_000, bytes_accessed=60_000_000, transcendentals=0),
    )(positions, charges, send_table, near_src, near_shift, freq, phase, shift)


def local(
    positions,
    charges,
    moment_freq,
    moment_phase,
    m2l_ops,
    child_parent_shift_matrix,
    send_leaf,
    send_count,
    far_src,
    far_class,
    near_src,
    near_shift,
    top_list,
    top_class,
):
    leaves = far_src.shape[0]
    in_bodies, in_rows, harmonic, left, near, moments, bodies = run_exchange(
        positions,
        charges.reshape(leaves, 1, WIDTH),
        send_leaf[0].T,
        near_src.T,
        near_shift.T,
        moment_freq,
        moment_phase[None],
        child_parent_shift_matrix,
        lax.axis_size("gx"),
        lax.axis_size("gy"),
    )
    result = run_finish(
        top_list, top_class, near_src.T, near_shift.T, far_src.T, far_class.T,
        m2l_ops, child_parent_shift_matrix, moments, in_rows,
        left, near, harmonic, bodies, in_bodies,
    )
    return result.reshape(leaves * WIDTH)


def solution(mesh):
    placed = (
        P(None, ("gx", "gy")),
        P(("gx", "gy")),
        P(),
        P(),
        P(),
        P(),
        P(("gx", "gy"), None, None),
        P(("gx", "gy"), None),
        P(("gx", "gy"), None),
        P(("gx", "gy"), None),
        P(("gx", "gy"), None),
        P(("gx", "gy"), None),
        P(("gx", "gy"), None),
        P(("gx", "gy"), None),
    )
    return jax.shard_map(
        local, mesh=mesh, in_specs=placed, out_specs=P(("gx", "gy")), check_vma=False
    )
```

```python
import functools
import math

import jax
import jax.numpy as jnp
from jax import lax
from jax.experimental import pallas as pl
from jax.experimental.pallas import tpu as pltpu
from jax.sharding import PartitionSpec as P

F32 = jnp.float32
BF16 = jnp.bfloat16
SOFTENING = 0.01
LEAVES = 64
WIDTH = 512
KPAD = 128
GROUPS = 48
UNROLL = 8
COS = (1.0, -19.73920440673828, 64.93911743164062, -85.45011138916016, 60.16743087768555, -25.96688461303711, 6.527706146240234)


def split2(a):
    high = a.astype(BF16)
    return high, (a - high.astype(F32)).astype(BF16)


def split3(a):
    high = a.astype(BF16).astype(F32)
    rest = a - high
    middle = rest.astype(BF16).astype(F32)
    return high, middle, rest - middle


def dot_nt(a, b):
    return lax.dot_general(a, b, (((1,), (1,)), ((), ())), preferred_element_type=F32)


def dot_nn(a, b):
    return jnp.dot(a, b, preferred_element_type=F32)


def dot3(dot, a, b):
    a_high, a_low = split2(a)
    b_high, b_low = split2(b)
    return dot(a_high, b_high) + (dot(a_high, b_low) + dot(a_low, b_high))


def pad8(record):
    return jnp.concatenate([record, jnp.zeros((4, record.shape[1]), F32)], axis=0)


def right_side(body, centre):
    row = lax.broadcasted_iota(jnp.int32, body.shape, 0)
    point = jnp.where(row < 3, body - centre, 0.0)
    norm = jnp.sum(point * point, axis=0, keepdims=True) + SOFTENING
    high, middle, low = split3(jnp.where(row == 3, norm, -2.0 * point))
    high_one = jnp.where(row == 3, 1.0, high)
    middle_one = jnp.where(row == 3, 1.0, middle)
    return jnp.concatenate([high, middle, high_one, low, high_one, middle_one], axis=0).astype(BF16)


def left_side(body):
    row = lax.broadcasted_iota(jnp.int32, body.shape, 0)
    point = jnp.where(row < 3, body - 0.5, 0.0)
    norm = jnp.sum(point * point, axis=0, keepdims=True)
    high, middle, low = split3(jnp.where(row == 3, norm, point))
    one = jnp.where(row == 3, 1.0, high)
    return jnp.concatenate(
        [
            one,
            one,
            jnp.where(row == 3, high, middle),
            one,
            jnp.where(row == 3, middle, low),
            jnp.where(row == 3, low, middle),
        ],
        axis=0,
    )


def phase_weights(waves):
    waves = pad8(waves)
    row = lax.broadcasted_iota(jnp.int32, waves.shape, 0)
    freq = jnp.where(row < 3, waves, 0.0)
    turn = jnp.sum(jnp.where(row < 3, 0.5 * waves, waves), axis=0, keepdims=True)
    turn = turn - jnp.round(turn)
    high, middle, low = split3(jnp.where(row == 3, turn, -0.5 * freq))
    plain = jnp.where(row == 3, 0.0, high)
    groups = jnp.concatenate(
        [
            plain,
            plain,
            jnp.where(row == 3, high, middle),
            plain,
            jnp.where(row == 3, middle, low),
            jnp.where(row == 3, low, middle),
        ],
        axis=0,
    )
    return groups.T.astype(BF16)


def cosine_turns(turns):
    rest = turns - jnp.round(turns)
    square = rest * rest
    value = jnp.full_like(square, COS[-1])
    for coefficient in COS[-2::-1]:
        value = value * square + coefficient
    return value


def lane_fold(a):
    return (a[:, :128] + a[:, 128:256]) + (a[:, 256:384] + a[:, 384:])


def basis_leaf(body, weights):
    return cosine_turns(dot_nn(weights, right_side(body, 0.5)))


def upward(moments, shift_ref):
    grouped = moments.reshape(8, 8, KPAD).sum(axis=0)
    row = lax.broadcasted_iota(jnp.int32, grouped.shape, 0)
    total = jnp.zeros((8, KPAD), F32)
    for child in range(8):
        total = total + dot3(dot_nt, jnp.where(row == child, grouped, 0.0), shift_ref[child])
    return jnp.sum(total, axis=0, keepdims=True)


def offset_vector(code):
    return (
        (code % 3 - 1).astype(F32),
        (code // 3 % 3 - 1).astype(F32),
        (code // 9 - 1).astype(F32),
    )


def source_right(body, shift):
    row = lax.broadcasted_iota(jnp.int32, body.shape, 0)
    shift_x, shift_y, shift_z = offset_vector(shift)
    centre = 0.5 - jnp.where(row == 0, shift_x, jnp.where(row == 1, shift_y, shift_z))
    return right_side(body, centre)


def pair_rows(left, right, charge, start, size):
    value = charge * lax.rsqrt(dot_nn(left[start : start + size], right))
    return lane_fold(value)


def near_fields(near_src, near_shift):
    source = near_src[...]
    column = lax.broadcasted_iota(jnp.int32, source.shape, 0)
    own = (source >= 0) & (source < LEAVES) & (column > 0)
    first_own = jnp.min(jnp.where(own, column.astype(F32), 8.0), axis=0, keepdims=True)
    taken = column.astype(F32) == first_own
    wanted = (source >= 0) & (column > 0) & jnp.logical_not(taken)
    word = (source + near_shift[...] * 65536 + (1 << 21)).astype(F32)
    return word, taken, wanted, source


def near_list(near_src, near_shift, listed):
    word, _, wanted, source = near_fields(near_src, near_shift)
    word = word + (source * 63 + lax.broadcasted_iota(jnp.int32, source.shape, 1)).astype(F32)
    mark = jnp.where(wanted, 1.0, 0.0)
    before = lax.broadcasted_iota(jnp.int32, (LEAVES, LEAVES), 0)
    before = before < lax.broadcasted_iota(jnp.int32, (LEAVES, LEAVES), 1)
    place = dot_nn(mark.astype(BF16), jnp.where(before, 1.0, 0.0).astype(BF16))
    totals = jnp.sum(mark, axis=1, keepdims=True)
    row = lax.broadcasted_iota(jnp.int32, (8, LEAVES), 0)
    for column in range(8):
        place = place + jnp.where(row > column, totals[column : column + 1], 0.0)
    place = jnp.where(wanted, place, -1.0).astype(jnp.int32)
    parts = split3(word)
    low_row = lax.broadcasted_iota(jnp.int32, (LEAVES, LEAVES), 0)
    codes = jnp.zeros((8, LEAVES), F32)
    for column in range(8):
        at = place[column : column + 1]
        low = jnp.where(low_row == (at & 63), 1.0, 0.0).astype(BF16)
        for part in parts:
            high = jnp.where(row == (at >> 6), part[column : column + 1], 0.0).astype(BF16)
            codes = codes + dot_nt(high, low)
    number = jnp.broadcast_to(jnp.sum(totals, axis=0, keepdims=True), (8, 128))
    listed[...] = number.astype(jnp.int32)
    listed[:, :LEAVES] = codes.astype(jnp.int32)


def pad_into(padded, ops):
    size, classes, width = ops.shape
    flat = ops.reshape(size * classes, width)
    padded[...] = jnp.zeros_like(padded)
    for place in range(classes):
        padded[place, :size, :width] = flat[pl.ds(place, size, stride=classes), :]


def local_expansions(pool_moments, m2l, shift, table, far_index, top_class, expansions):
    rows = pool_moments.shape[0]
    pool_high, pool_low = split2(pool_moments[...])
    for pair in range(8):
        op_high, op_low = split2(m2l[2 * pair : 2 * pair + 2].reshape(256, KPAD))
        moved = dot_nt(pool_high, op_high) + (dot_nt(pool_high, op_low) + dot_nt(pool_low, op_high))
        table[2 * pair * rows : (2 * pair + 1) * rows] = moved[:, :KPAD]
        table[(2 * pair + 1) * rows : (2 * pair + 2) * rows] = moved[:, KPAD:]
    table[16 * rows : 16 * rows + 8] = jnp.zeros((8, KPAD), F32)

    def tree(parts):
        while len(parts) > 1:
            parts = [a + b for a, b in zip(parts[::2], parts[1::2])]
        return parts[0]

    top_local = tree(
        [table[pl.ds(top_class[0, e] * rows + (rows - 32 + e), 1), :] for e in range(32)]
    )
    top_rows = jnp.broadcast_to(top_local, (8, KPAD))
    row = lax.broadcasted_iota(jnp.int32, (8, KPAD), 0)
    down = jnp.zeros((8, KPAD), F32)
    for child in range(8):
        down = jnp.where(row == child, dot3(dot_nn, top_rows, shift[child]), down)

    def gather(leaf, carry):
        expansions[pl.ds(leaf, 1), :] = tree(
            [table[pl.ds(far_index[e, leaf], 1), :] for e in range(32)]
        )
        return carry

    lax.fori_loop(0, LEAVES, gather, 0)
    return (expansions[...].reshape(8, 8, KPAD) + down[None]).reshape(LEAVES, KPAD)


def finish_kernel(
    top_list, top_class,
    near_src, near_shift, far_src, far_class, m2l_ops, shift_ops, own_moments, in_rows,
    left_hbm, near_hbm, harmonic_hbm, bodies_hbm, in_bodies_hbm,
    out,
    pool, left, near, harmonic, pool_moments, table, expansions, m2l, shift,
    listed, far_rows, codes, far_index, sems,
):
    slots = in_bodies_hbm.shape[0]
    copies = [
        pltpu.make_async_copy(source, target, sems.at[place])
        for place, (source, target) in enumerate(
            (
                (left_hbm, left),
                (bodies_hbm, pool.at[pl.ds(0, LEAVES)]),
                (in_bodies_hbm, pool.at[pl.ds(LEAVES, slots)]),
                (near_hbm, near),
                (harmonic_hbm, harmonic),
            )
        )
    ]
    for copy in copies:
        copy.start()
    entry_rows = 16 * (LEAVES + slots + 32)
    source = far_src[...]
    far_rows[...] = jnp.zeros_like(far_rows)
    far_rows[:, :LEAVES] = jnp.where(
        source >= 0, far_class[...] * (entry_rows // 16) + source, entry_rows
    )
    near_list(near_src, near_shift, listed)
    words = [
        pltpu.make_async_copy(far_rows, far_index, sems.at[5]),
        pltpu.make_async_copy(listed, codes, sems.at[6]),
    ]
    for copy in words:
        copy.start()
    pad_into(m2l, m2l_ops)
    pad_into(shift, shift_ops)
    rows = LEAVES + slots
    pool_moments[:LEAVES] = own_moments[...]
    fine = in_rows.shape[1] // 3
    for peer in range(in_rows.shape[0]):
        start = LEAVES + 2 * fine * peer
        pool_moments[start : start + 2 * fine] = in_rows[peer, : 2 * fine]
    for e in range(32):
        owner = top_list[0, e]
        pool_moments[rows + e : rows + e + 1, :] = in_rows[
            owner // fine, pl.ds(2 * fine + lax.rem(owner, fine), 1), :
        ]
    for copy in words:
        copy.wait()
    local = local_expansions(pool_moments, m2l, shift, table, far_index, top_class, expansions)
    local_columns = jnp.concatenate([local, jnp.zeros((KPAD - LEAVES, KPAD), F32)], axis=0).T

    for copy in copies[:4]:
        copy.wait()

    def near_step(group, carry):
        for member in range(UNROLL):
            code = codes[group >> 3, (group & 7) * UNROLL + member]
            target = code & 63
            source = (code >> 6) & 1023
            live = (code >> 21).astype(F32)
            body = pad8(pool[source])
            right = source_right(body, (code >> 16) & 31)
            charge = body[3:4] * live
            for start in range(0, WIDTH, 128):
                near[target, start : start + 128] += pair_rows(
                    left.at[target][:, :GROUPS], right, charge, start, 128
                )
        return carry

    lax.fori_loop(0, (codes[0, LEAVES] + UNROLL - 1) // UNROLL, near_step, 0)
    copies[4].wait()
    ones = jnp.ones((8, 128), BF16)

    def far_step(group, columns):
        for member in range(8):
            leaf = group * 8 + member
            product = harmonic[leaf] * columns[:, member : member + 1]
            far = jnp.sum(product, axis=0, keepdims=True)
            near_high, near_low = split2(near[leaf])
            total = dot_nt(ones, near_high) + dot_nt(ones, near_low)
            out[leaf] = total[:1] + far
        return pltpu.roll(columns, KPAD - 8, 1)

    lax.fori_loop(0, LEAVES // 8, far_step, local_columns)


SMEM = pl.BlockSpec(memory_space=pltpu.SMEM)
VMEM = pl.BlockSpec(memory_space=pltpu.VMEM)
ANY = pl.BlockSpec(memory_space=pl.ANY)


def run_finish(
    top_list, top_class, near_src, near_shift, far_src, far_class, m2l, shift, moments, in_rows,
    left, near, harmonic, bodies, in_bodies,
):
    slots = in_bodies.shape[0]
    rows = LEAVES + slots + 32
    return pl.pallas_call(
        finish_kernel,
        out_shape=jax.ShapeDtypeStruct((LEAVES, 1, WIDTH), F32),
        in_specs=[SMEM] * 2 + [VMEM] * 8 + [ANY] * 5,
        out_specs=VMEM,
        scratch_shapes=[
            pltpu.VMEM((LEAVES + slots, 4, WIDTH), F32),
            pltpu.VMEM((LEAVES, WIDTH, 128), BF16),
            pltpu.VMEM((LEAVES, WIDTH, 128), F32),
            pltpu.VMEM((LEAVES, KPAD, WIDTH), F32),
            pltpu.VMEM((rows, KPAD), F32),
            pltpu.VMEM((16 * rows + 8, KPAD), F32),
            pltpu.VMEM((LEAVES, KPAD), F32),
            pltpu.VMEM((16, KPAD, KPAD), F32),
            pltpu.VMEM((8, KPAD, KPAD), F32),
            pltpu.VMEM((8, 128), jnp.int32),
            pltpu.VMEM((32, 128), jnp.int32),
            pltpu.SMEM((8, 128), jnp.int32),
            pltpu.SMEM((32, 128), jnp.int32),
            pltpu.SemaphoreType.DMA((7,)),
        ],
        compiler_params=pltpu.CompilerParams(vmem_limit_bytes=62 << 20),
        cost_estimate=pl.CostEstimate(flops=60_000_000_000, bytes_accessed=40_000_000, transcendentals=0),
    )(
        top_list, top_class, near_src, near_shift, far_src, far_class, m2l, shift, moments, in_rows,
        left, near, harmonic, bodies, in_bodies,
    )


def exchange_kernel(
    positions, charges, send_table, near_src, near_shift, freq, phase, shift_ops,
    in_bodies, in_rows, harmonic_out, left_out, near_out, moments, bodies,
    r1, r2, r3, l1, l2, l3, opposite,
    packs, harmonic, left, near, shift, waves, transposed, column_rows, row_pack,
    table, tables, table_words, own_table, pair_words, pairs,
    ring_send, ring_recv, small_send, small_recv, plane_send, plane_recv, local_sems, out_sems,
):
    gx, gy = lax.axis_index("gx"), lax.axis_index("gy")
    coarse, fine = row_pack.shape[0], column_rows.shape[0]
    right = {"gy": lax.rem(gy + 1, fine)}
    back = {"gy": lax.rem(gy + fine - 1, fine)}
    half = LEAVES // 2

    def build(quad, carry):
        for member in range(4):
            leaf = quad * 4 + member
            place = pl.ds(pl.multiple_of(leaf * WIDTH, WIDTH), WIDTH)
            bodies[leaf] = jnp.concatenate([positions[:, place], charges[leaf]], axis=0)
        return carry

    lax.fori_loop(0, LEAVES // 4, build, 0)
    table[...] = jnp.zeros_like(table)
    table[: send_table.shape[0], :] = send_table[...]
    barrier = pltpu.get_barrier_semaphore()

    def greet_plane(j, carry):
        pl.semaphore_signal(barrier, inc=1, device_id={"gx": lax.rem(gx + j, coarse)})
        return carry

    lax.fori_loop(1, coarse, greet_plane, 0)
    for k in range(1, fine):
        pl.semaphore_signal(barrier, inc=1, device_id={"gy": lax.rem(gy + k, fine)})
    pl.semaphore_wait(barrier, coarse + fine - 2)

    def remote(source, target, send, recv, device):
        copy = pltpu.make_async_remote_copy(
            src_ref=source, dst_ref=target, send_sem=send, recv_sem=recv, device_id=device
        )
        copy.start()
        return copy

    def ring(step):
        if step == 4:
            return (
                remote(r3.at[pl.ds(0, half)], opposite.at[pl.ds(0, half)],
                       ring_send.at[6], ring_recv.at[6], right),
                remote(l3.at[pl.ds(half, half)], opposite.at[pl.ds(half, half)],
                       ring_send.at[7], ring_recv.at[7], back),
            )
        sources = ((bodies, bodies), (r1, l1), (r2, l2))[step - 1]
        targets = ((r1, l1), (r2, l2), (r3, l3))[step - 1]
        slot = 2 * (step - 1)
        return (
            remote(sources[0], targets[0], ring_send.at[slot], ring_recv.at[slot], right),
            remote(sources[1], targets[1], ring_send.at[slot + 1], ring_recv.at[slot + 1], back),
        )

    for k in range(1, fine):
        there = lax.rem(gy + k, fine)
        remote(table, tables.at[k], small_send.at[0], small_recv.at[0], {"gy": there})
    first = ring(1)
    own_words = pltpu.make_async_copy(table, own_table, local_sems.at[0])
    own_words.start()
    own_words.wait()

    def pack(block, offset, words):
        there = lax.rem(gy + fine - offset, fine)
        buffer = packs.at[offset]
        place = pl.ds((gx * fine + there) * 2, 2)

        def one(quad, carry):
            for part in range(4):
                peer = quad * 4 + part
                for slot in range(2):
                    buffer[peer, slot] = block[words[slot, peer * fine + gy]]
            return carry

        lax.fori_loop(0, coarse // 4, one, 0)

        def push(j, carry):
            peer = lax.rem(gx + j, coarse)
            remote(buffer.at[peer], in_bodies.at[place], plane_send.at[0], plane_recv.at[0],
                   {"gx": peer})
            return carry

        lax.fori_loop(1, coarse, push, 0)
        keep = pltpu.make_async_copy(buffer.at[gx], in_bodies.at[place], local_sems.at[1 + offset])
        keep.start()
        return keep

    kept = [pack(bodies, 0, own_table)]

    word, taken, _, _ = near_fields(near_src, near_shift)
    pair_words[...] = jnp.zeros_like(pair_words)
    pair_words[:1, :LEAVES] = word[:1].astype(jnp.int32)
    pair_words[1:2, :LEAVES] = jnp.sum(
        jnp.where(taken, word, 0.0), axis=0, keepdims=True
    ).astype(jnp.int32)
    words = pltpu.make_async_copy(pair_words, pairs, local_sems.at[0])
    words.start()
    words.wait()
    pad_into(shift, shift_ops)
    waves[...] = jnp.zeros_like(waves)
    waves[:3, : freq.shape[1]] = freq[...]
    waves[3:4, : freq.shape[1]] = phase[...] * (0.5 / math.pi)
    weights = phase_weights(waves[...])
    lane = lax.broadcasted_iota(jnp.int32, (KPAD, KPAD), 1)
    transposed[...] = jnp.zeros_like(transposed)

    def feature_step(quad, carry):
        for member in range(4):
            leaf = quad * 4 + member
            body = pad8(bodies[leaf])
            basis = basis_leaf(body, weights)
            harmonic[leaf] = basis
            column = jnp.sum(lane_fold(basis * body[3:4]), axis=1, keepdims=True)
            transposed[...] = jnp.where(lane == leaf, column, transposed[...])
            left[leaf, :, :GROUPS] = left_side(body).T.astype(BF16)
        return carry

    def near_step(quad, carry):
        for member in range(4):
            leaf = quad * 4 + member
            sides = []
            for entry in range(2):
                code = pairs[entry, leaf]
                body = pad8(bodies[code & 63])
                charge = body[3:4] * (code >> 21).astype(F32)
                sides.append((source_right(body, (code >> 16) & 31), charge))
            rows = left[leaf][:, :GROUPS]
            for start in range(0, WIDTH, 128):
                near[leaf, start : start + 128] = sum(
                    pair_rows(rows, side, charge, start, 128) for side, charge in sides
                )
        return carry

    left[...] = jnp.zeros_like(left)
    lax.fori_loop(0, half // 4, feature_step, 0)

    first[0].wait_recv()
    first[1].wait_recv()
    second = ring(2)
    sent_tables = tables.at[pl.ds(1, fine - 1)]
    pltpu.make_async_copy(sent_tables, sent_tables, small_recv.at[0]).wait()
    words = pltpu.make_async_copy(
        sent_tables, table_words.at[pl.ds(1, fine - 1)], local_sems.at[0]
    )
    words.start()
    words.wait()
    kept += [pack(r1, 1, table_words.at[1]), pack(l1, fine - 1, table_words.at[fine - 1])]
    lax.fori_loop(half // 4, LEAVES // 4, feature_step, 0)

    outs = [
        pltpu.make_async_copy(harmonic, harmonic_out, out_sems.at[0]),
        pltpu.make_async_copy(left, left_out, out_sems.at[1]),
    ]
    for copy in outs:
        copy.start()
    own = transposed[...].T[:LEAVES]
    moments[...] = own
    column_rows[0, :LEAVES] = own
    column_rows[0, LEAVES:] = jnp.broadcast_to(upward(own, shift), (8, KPAD))
    for k in range(1, fine):
        remote(column_rows.at[0], column_rows.at[k], small_send.at[1], small_recv.at[1],
               {"gy": lax.rem(gy + k, fine)})

    second[0].wait_recv()
    second[1].wait_recv()
    third = ring(3)
    kept += [pack(r2, 2, table_words.at[2]), pack(l2, fine - 2, table_words.at[fine - 2])]
    lax.fori_loop(0, half // 4, near_step, 0)
    outs.append(
        pltpu.make_async_copy(near.at[pl.ds(0, half)], near_out.at[pl.ds(0, half)], out_sems.at[2])
    )
    outs[-1].start()

    third[0].wait_recv()
    third[1].wait_recv()
    fourth = ring(4)
    kept += [pack(r3, 3, table_words.at[3]), pack(l3, fine - 3, table_words.at[fine - 3])]

    others = column_rows.at[pl.ds(1, fine - 1)]
    pltpu.make_async_copy(others, others, small_recv.at[1]).wait()
    for offset in range(fine):
        there = lax.rem(gy + fine - offset, fine)

        def pick(quad, carry):
            for part in range(4):
                peer = quad * 4 + part
                for slot in range(2):
                    row = (table_words.at[offset] if offset else own_table)[
                        slot, peer * fine + gy
                    ]
                    row_pack[peer, pl.ds(there * 2 + slot, 1), :] = column_rows[
                        offset, pl.ds(row, 1), :
                    ]
                row_pack[peer, pl.ds(2 * fine + there, 1), :] = column_rows[
                    offset, LEAVES : LEAVES + 1, :
                ]
            return carry

        lax.fori_loop(0, coarse // 4, pick, 0)

    def push_rows(j, carry):
        peer = lax.rem(gx + j, coarse)
        remote(row_pack.at[peer], in_rows.at[gx], plane_send.at[1], plane_recv.at[1], {"gx": peer})
        return carry

    lax.fori_loop(1, coarse, push_rows, 0)
    keep = pltpu.make_async_copy(row_pack.at[gx], in_rows.at[gx], local_sems.at[0])
    keep.start()
    kept.append(keep)

    fourth[0].wait_recv()
    fourth[1].wait_recv()
    kept += [pack(opposite, fine // 2, table_words.at[fine // 2])]

    lax.fori_loop(half // 4, LEAVES // 4, near_step, 0)
    outs.append(
        pltpu.make_async_copy(
            near.at[pl.ds(half, half)], near_out.at[pl.ds(half, half)], out_sems.at[3]
        )
    )
    outs[-1].start()

    for copy in kept + outs:
        copy.wait()
    for copy in first + second + third + fourth:
        copy.wait_send()
    pltpu.make_async_copy(sent_tables, sent_tables, small_send.at[0]).wait()
    pltpu.make_async_copy(others, others, small_send.at[1]).wait()
    sent = in_bodies.at[pl.ds(0, (coarse - 1) * fine * 2)]
    pltpu.make_async_copy(sent, sent, plane_send.at[0]).wait()
    pltpu.make_async_copy(sent, sent, plane_recv.at[0]).wait()
    sent = in_rows.at[pl.ds(0, coarse - 1)]
    pltpu.make_async_copy(sent, sent, plane_send.at[1]).wait()
    pltpu.make_async_copy(sent, sent, plane_recv.at[1]).wait()


def run_exchange(positions, charges, send_table, near_src, near_shift, freq, phase, shift, coarse, fine):
    block = pltpu.VMEM((LEAVES, 4, WIDTH), F32)
    return pl.pallas_call(
        exchange_kernel,
        out_shape=[
            jax.ShapeDtypeStruct((coarse * fine * 2, 4, WIDTH), F32),
            jax.ShapeDtypeStruct((coarse, 3 * fine, KPAD), F32),
            jax.ShapeDtypeStruct((LEAVES, KPAD, WIDTH), F32),
            jax.ShapeDtypeStruct((LEAVES, WIDTH, 128), BF16),
            jax.ShapeDtypeStruct((LEAVES, WIDTH, 128), F32),
            jax.ShapeDtypeStruct((LEAVES, KPAD), F32),
            jax.ShapeDtypeStruct((LEAVES, 4, WIDTH), F32),
        ],
        in_specs=[VMEM] * 8,
        out_specs=[ANY] * 5 + [VMEM] * 2,
        scratch_shapes=[block] * 7
        + [
            pltpu.VMEM((fine, coarse, 2, 4, WIDTH), F32),
            pltpu.VMEM((LEAVES, KPAD, WIDTH), F32),
            pltpu.VMEM((LEAVES, WIDTH, 128), BF16),
            pltpu.VMEM((LEAVES, WIDTH, 128), F32),
            pltpu.VMEM((8, KPAD, KPAD), F32),
            pltpu.VMEM((4, KPAD), F32),
            pltpu.VMEM((KPAD, KPAD), F32),
            pltpu.VMEM((fine, LEAVES + 8, KPAD), F32),
            pltpu.VMEM((coarse, 3 * fine, KPAD), F32),
            pltpu.VMEM((8, coarse * fine), jnp.int32),
            pltpu.VMEM((fine, 8, coarse * fine), jnp.int32),
            pltpu.SMEM((fine, 8, coarse * fine), jnp.int32),
            pltpu.SMEM((8, coarse * fine), jnp.int32),
            pltpu.VMEM((8, 128), jnp.int32),
            pltpu.SMEM((8, 128), jnp.int32),
            pltpu.SemaphoreType.DMA((8,)),
            pltpu.SemaphoreType.DMA((8,)),
            pltpu.SemaphoreType.DMA((2,)),
            pltpu.SemaphoreType.DMA((2,)),
            pltpu.SemaphoreType.DMA((2,)),
            pltpu.SemaphoreType.DMA((2,)),
            pltpu.SemaphoreType.DMA((1 + fine,)),
            pltpu.SemaphoreType.DMA((4,)),
        ],
        compiler_params=pltpu.CompilerParams(
            vmem_limit_bytes=62 << 20, collective_id=0, has_side_effects=True
        ),
        cost_estimate=pl.CostEstimate(flops=40_000_000_000, bytes_accessed=60_000_000, transcendentals=0),
    )(positions, charges, send_table, near_src, near_shift, freq, phase, shift)


def local(
    positions,
    charges,
    moment_freq,
    moment_phase,
    m2l_ops,
    child_parent_shift_matrix,
    send_leaf,
    send_count,
    far_src,
    far_class,
    near_src,
    near_shift,
    top_list,
    top_class,
):
    leaves = far_src.shape[0]
    in_bodies, in_rows, harmonic, left, near, moments, bodies = run_exchange(
        positions,
        charges.reshape(leaves, 1, WIDTH),
        send_leaf[0].T,
        near_src.T,
        near_shift.T,
        moment_freq,
        moment_phase[None],
        child_parent_shift_matrix.transpose(1, 0, 2),
        lax.axis_size("gx"),
        lax.axis_size("gy"),
    )
    result = run_finish(
        top_list, top_class, near_src.T, near_shift.T, far_src.T, far_class.T,
        m2l_ops.transpose(1, 0, 2), child_parent_shift_matrix.transpose(1, 0, 2), moments, in_rows,
        left, near, harmonic, bodies, in_bodies,
    )
    return result.reshape(leaves * WIDTH)


def solution(mesh):
    placed = (
        P(None, ("gx", "gy")),
        P(("gx", "gy")),
        P(),
        P(),
        P(),
        P(),
        P(("gx", "gy"), None, None),
        P(("gx", "gy"), None),
        P(("gx", "gy"), None),
        P(("gx", "gy"), None),
        P(("gx", "gy"), None),
        P(("gx", "gy"), None),
        P(("gx", "gy"), None),
        P(("gx", "gy"), None),
    )
    return jax.shard_map(
        local, mesh=mesh, in_specs=placed, out_specs=P(("gx", "gy")), check_vma=False
    )
```

```python
import functools
import math

import jax
import jax.numpy as jnp
from jax import lax
from jax.experimental import pallas as pl
from jax.experimental.pallas import tpu as pltpu
from jax.sharding import PartitionSpec as P

F32 = jnp.float32
BF16 = jnp.bfloat16
SOFTENING = 0.01
LEAVES = 64
WIDTH = 512
KPAD = 128
GROUPS = 48
UNROLL = 8
COS = (1.0, -19.73920440673828, 64.93911743164062, -85.45011138916016, 60.16743087768555, -25.96688461303711, 6.527706146240234)


def split2(a):
    high = a.astype(BF16)
    return high, (a - high.astype(F32)).astype(BF16)


def split3(a):
    high = a.astype(BF16).astype(F32)
    rest = a - high
    middle = rest.astype(BF16).astype(F32)
    return high, middle, rest - middle


def dot_nt(a, b):
    return lax.dot_general(a, b, (((1,), (1,)), ((), ())), preferred_element_type=F32)


def dot_nn(a, b):
    return jnp.dot(a, b, preferred_element_type=F32)


def dot3(dot, a, b):
    a_high, a_low = split2(a)
    b_high, b_low = split2(b)
    return dot(a_high, b_high) + (dot(a_high, b_low) + dot(a_low, b_high))


def pad8(record):
    return jnp.concatenate([record, jnp.zeros((4, record.shape[1]), F32)], axis=0)


def right_side(body, centre):
    row = lax.broadcasted_iota(jnp.int32, body.shape, 0)
    point = jnp.where(row < 3, body - centre, 0.0)
    norm = jnp.sum(point * point, axis=0, keepdims=True) + SOFTENING
    high, middle, low = split3(jnp.where(row == 3, norm, -2.0 * point))
    high_one = jnp.where(row == 3, 1.0, high)
    middle_one = jnp.where(row == 3, 1.0, middle)
    return jnp.concatenate([high, middle, high_one, low, high_one, middle_one], axis=0).astype(BF16)


def left_side(body):
    row = lax.broadcasted_iota(jnp.int32, body.shape, 0)
    point = jnp.where(row < 3, body - 0.5, 0.0)
    norm = jnp.sum(point * point, axis=0, keepdims=True)
    high, middle, low = split3(jnp.where(row == 3, norm, point))
    one = jnp.where(row == 3, 1.0, high)
    return jnp.concatenate(
        [
            one,
            one,
            jnp.where(row == 3, high, middle),
            one,
            jnp.where(row == 3, middle, low),
            jnp.where(row == 3, low, middle),
        ],
        axis=0,
    )


def phase_weights(waves):
    waves = pad8(waves)
    row = lax.broadcasted_iota(jnp.int32, waves.shape, 0)
    freq = jnp.where(row < 3, waves, 0.0)
    turn = jnp.sum(jnp.where(row < 3, 0.5 * waves, waves), axis=0, keepdims=True)
    turn = turn - jnp.round(turn)
    high, middle, low = split3(jnp.where(row == 3, turn, -0.5 * freq))
    plain = jnp.where(row == 3, 0.0, high)
    groups = jnp.concatenate(
        [
            plain,
            plain,
            jnp.where(row == 3, high, middle),
            plain,
            jnp.where(row == 3, middle, low),
            jnp.where(row == 3, low, middle),
        ],
        axis=0,
    )
    return groups.T.astype(BF16)


def cosine_turns(turns):
    rest = turns - jnp.round(turns)
    square = rest * rest
    value = jnp.full_like(square, COS[-1])
    for coefficient in COS[-2::-1]:
        value = value * square + coefficient
    return value


def lane_fold(a):
    return (a[:, :128] + a[:, 128:256]) + (a[:, 256:384] + a[:, 384:])


def basis_leaf(body, weights):
    return cosine_turns(dot_nn(weights, right_side(body, 0.5)))


def upward(moments, shift_ref):
    grouped = moments.reshape(8, 8, KPAD).sum(axis=0)
    row = lax.broadcasted_iota(jnp.int32, grouped.shape, 0)
    total = jnp.zeros((8, KPAD), F32)
    for child in range(8):
        total = total + dot3(dot_nt, jnp.where(row == child, grouped, 0.0), shift_ref[child])
    return jnp.sum(total, axis=0, keepdims=True)


def offset_vector(code):
    return (
        (code % 3 - 1).astype(F32),
        (code // 3 % 3 - 1).astype(F32),
        (code // 9 - 1).astype(F32),
    )


def source_right(body, shift):
    row = lax.broadcasted_iota(jnp.int32, body.shape, 0)
    shift_x, shift_y, shift_z = offset_vector(shift)
    centre = 0.5 - jnp.where(row == 0, shift_x, jnp.where(row == 1, shift_y, shift_z))
    return right_side(body, centre)


def pair_rows(left, right, charge, start, size):
    value = charge * lax.rsqrt(dot_nn(left[start : start + size], right))
    return lane_fold(value)


def near_fields(near_src, near_shift):
    source = near_src[...]
    column = lax.broadcasted_iota(jnp.int32, source.shape, 0)
    own = (source >= 0) & (source < LEAVES) & (column > 0)
    first_own = jnp.min(jnp.where(own, column.astype(F32), 8.0), axis=0, keepdims=True)
    taken = column.astype(F32) == first_own
    wanted = (source >= 0) & (column > 0) & jnp.logical_not(taken)
    word = (source + near_shift[...] * 65536 + (1 << 21)).astype(F32)
    return word, taken, wanted, source


def near_list(near_src, near_shift, listed):
    word, _, wanted, source = near_fields(near_src, near_shift)
    lane = lax.broadcasted_iota(jnp.int32, source.shape, 1)
    slot = source - LEAVES
    back = (lax.axis_index("gy") - (slot >> 1)) & 7
    position = jnp.where(
        back == 0, 0, jnp.where(back < 4, 2 * back - 1, jnp.where(back == 4, 7, 16 - 2 * back))
    )
    place = jnp.where(slot < 0, source, LEAVES + (slot >> 4) * 16 + position * 2 + (slot & 1))
    word = word + (place * 64 - source + lane).astype(F32)
    mark = jnp.where(wanted, 1.0, 0.0)
    first = lax.broadcasted_iota(jnp.int32, (LEAVES, LEAVES), 0)
    second = lax.broadcasted_iota(jnp.int32, (LEAVES, LEAVES), 1)
    same = (first >> 5) == (second >> 5)
    before = jnp.where(same & (first < second), 1.0, 0.0).astype(BF16)
    rank = dot_nn(mark.astype(BF16), before)
    totals = dot_nn(mark.astype(BF16), jnp.where(same, 1.0, 0.0).astype(BF16))
    row = lax.broadcasted_iota(jnp.int32, (8, LEAVES), 0)
    for column in range(8):
        rank = rank + jnp.where(row > column, totals[column : column + 1], 0.0)
    rank = rank.astype(jnp.int32) + (lane >> 5) * 256
    rank = jnp.where(wanted, rank, -1)
    parts = split3(word)
    codes = jnp.zeros((8, LEAVES), F32)
    for column in range(8):
        at = rank[column : column + 1]
        low = jnp.where(first == (at & 63), 1.0, 0.0).astype(BF16)
        for part in parts:
            high = jnp.where(row == (at >> 6), part[column : column + 1], 0.0).astype(BF16)
            codes = codes + dot_nt(high, low)
    number = jnp.broadcast_to(jnp.sum(totals, axis=0, keepdims=True), (8, LEAVES))
    listed[...] = jnp.concatenate([codes, number], axis=1).astype(jnp.int32)


def pad_into(padded, ops):
    size, classes, width = ops.shape
    flat = ops.reshape(size * classes, width)
    padded[...] = jnp.zeros_like(padded)
    for place in range(classes):
        padded[place, :size, :width] = flat[pl.ds(place, size, stride=classes), :]


def local_expansions(pool_moments, m2l, shift, table, far_index, top_class, expansions):
    rows = pool_moments.shape[0]
    pool_high, pool_low = split2(pool_moments[...])
    for pair in range(8):
        op_high, op_low = split2(m2l[2 * pair : 2 * pair + 2].reshape(256, KPAD))
        moved = dot_nt(pool_high, op_high) + (dot_nt(pool_high, op_low) + dot_nt(pool_low, op_high))
        table[2 * pair * rows : (2 * pair + 1) * rows] = moved[:, :KPAD]
        table[(2 * pair + 1) * rows : (2 * pair + 2) * rows] = moved[:, KPAD:]
    table[16 * rows : 16 * rows + 8] = jnp.zeros((8, KPAD), F32)

    def tree(parts):
        while len(parts) > 1:
            parts = [a + b for a, b in zip(parts[::2], parts[1::2])]
        return parts[0]

    top_local = tree(
        [table[pl.ds(top_class[0, e] * rows + (rows - 32 + e), 1), :] for e in range(32)]
    )
    top_rows = jnp.broadcast_to(top_local, (8, KPAD))
    row = lax.broadcasted_iota(jnp.int32, (8, KPAD), 0)
    down = jnp.zeros((8, KPAD), F32)
    for child in range(8):
        down = jnp.where(row == child, dot3(dot_nn, top_rows, shift[child]), down)

    def gather(leaf, carry):
        expansions[pl.ds(leaf, 1), :] = tree(
            [table[pl.ds(far_index[e, leaf], 1), :] for e in range(32)]
        )
        return carry

    lax.fori_loop(0, LEAVES, gather, 0)
    return (expansions[...].reshape(8, 8, KPAD) + down[None]).reshape(LEAVES, KPAD)


def finish_kernel(
    top_list, top_class,
    near_src, near_shift, far_src, far_class, m2l_ops, shift_ops, own_moments, in_rows,
    left_hbm, near_hbm, harmonic_hbm, bodies_hbm, in_bodies_hbm,
    out,
    pool, left, near, harmonic, pool_moments, table, expansions, m2l, shift,
    listed, far_rows, codes, far_index, sems,
):
    slots = in_bodies_hbm.shape[0]
    copies = [
        pltpu.make_async_copy(source, target, sems.at[place])
        for place, (source, target) in enumerate(
            (
                (left_hbm, left),
                (bodies_hbm, pool.at[pl.ds(0, LEAVES)]),
                (in_bodies_hbm, pool.at[pl.ds(LEAVES, slots)]),
                (near_hbm.at[pl.ds(0, LEAVES // 2)], near.at[pl.ds(0, LEAVES // 2)]),
                (
                    near_hbm.at[pl.ds(LEAVES // 2, LEAVES // 2)],
                    near.at[pl.ds(LEAVES // 2, LEAVES // 2)],
                ),
                (harmonic_hbm, harmonic),
            )
        )
    ]
    for copy in copies:
        copy.start()
    entry_rows = 16 * (LEAVES + slots + 32)
    source = far_src[...]
    far_rows[...] = jnp.zeros_like(far_rows)
    far_rows[:, :LEAVES] = jnp.where(
        source >= 0, far_class[...] * (entry_rows // 16) + source, entry_rows
    )
    near_list(near_src, near_shift, listed)
    words = [
        pltpu.make_async_copy(far_rows, far_index, sems.at[6]),
        pltpu.make_async_copy(listed, codes, sems.at[7]),
    ]
    for copy in words:
        copy.start()
    pad_into(m2l, m2l_ops)
    pad_into(shift, shift_ops)
    rows = LEAVES + slots
    pool_moments[:LEAVES] = own_moments[...]
    fine = in_rows.shape[1] // 3
    for peer in range(in_rows.shape[0]):
        start = LEAVES + 2 * fine * peer
        pool_moments[start : start + 2 * fine] = in_rows[peer, : 2 * fine]
    for e in range(32):
        owner = top_list[0, e]
        pool_moments[rows + e : rows + e + 1, :] = in_rows[
            owner // fine, pl.ds(2 * fine + lax.rem(owner, fine), 1), :
        ]
    for copy in words:
        copy.wait()
    local = local_expansions(pool_moments, m2l, shift, table, far_index, top_class, expansions)
    local_columns = jnp.concatenate([local, jnp.zeros((KPAD - LEAVES, KPAD), F32)], axis=0).T

    for copy in copies[:4]:
        copy.wait()

    def near_step(group, half):
        for member in range(UNROLL):
            code = codes[4 * half + (group >> 3), (group & 7) * UNROLL + member]
            target = code & 63
            source = (code >> 6) & 1023
            live = (code >> 21).astype(F32)
            body = pad8(pool[source])
            right = source_right(body, (code >> 16) & 31)
            charge = body[3:4] * live
            for start in range(0, WIDTH, 128):
                near[target, start : start + 128] += pair_rows(
                    left.at[target][:, :GROUPS], right, charge, start, 128
                )
        return half

    lax.fori_loop(0, (codes[0, LEAVES] + UNROLL - 1) // UNROLL, near_step, 0)
    copies[4].wait()
    lax.fori_loop(0, (codes[0, LEAVES + 32] + UNROLL - 1) // UNROLL, near_step, 1)
    copies[5].wait()
    ones = jnp.ones((8, 128), BF16)

    def far_step(group, columns):
        for member in range(8):
            leaf = group * 8 + member
            product = harmonic[leaf] * columns[:, member : member + 1]
            far = jnp.sum(product, axis=0, keepdims=True)
            near_high, near_low = split2(near[leaf])
            total = dot_nt(ones, near_high) + dot_nt(ones, near_low)
            out[leaf] = total[:1] + far
        return pltpu.roll(columns, KPAD - 8, 1)

    lax.fori_loop(0, LEAVES // 8, far_step, local_columns)


SMEM = pl.BlockSpec(memory_space=pltpu.SMEM)
VMEM = pl.BlockSpec(memory_space=pltpu.VMEM)
ANY = pl.BlockSpec(memory_space=pl.ANY)


def run_finish(
    top_list, top_class, near_src, near_shift, far_src, far_class, m2l, shift, moments, in_rows,
    left, near, harmonic, bodies, in_bodies,
):
    slots = in_bodies.shape[0]
    rows = LEAVES + slots + 32
    return pl.pallas_call(
        finish_kernel,
        out_shape=jax.ShapeDtypeStruct((LEAVES, 1, WIDTH), F32),
        in_specs=[SMEM] * 2 + [VMEM] * 8 + [ANY] * 5,
        out_specs=VMEM,
        scratch_shapes=[
            pltpu.VMEM((LEAVES + slots, 4, WIDTH), F32),
            pltpu.VMEM((LEAVES, WIDTH, 128), BF16),
            pltpu.VMEM((LEAVES, WIDTH, 128), F32),
            pltpu.VMEM((LEAVES, KPAD, WIDTH), F32),
            pltpu.VMEM((rows, KPAD), F32),
            pltpu.VMEM((16 * rows + 8, KPAD), F32),
            pltpu.VMEM((LEAVES, KPAD), F32),
            pltpu.VMEM((16, KPAD, KPAD), F32),
            pltpu.VMEM((8, KPAD, KPAD), F32),
            pltpu.VMEM((8, 128), jnp.int32),
            pltpu.VMEM((32, 128), jnp.int32),
            pltpu.SMEM((8, 128), jnp.int32),
            pltpu.SMEM((32, 128), jnp.int32),
            pltpu.SemaphoreType.DMA((8,)),
        ],
        compiler_params=pltpu.CompilerParams(vmem_limit_bytes=62 << 20),
        cost_estimate=pl.CostEstimate(flops=60_000_000_000, bytes_accessed=40_000_000, transcendentals=0),
    )(
        top_list, top_class, near_src, near_shift, far_src, far_class, m2l, shift, moments, in_rows,
        left, near, harmonic, bodies, in_bodies,
    )


def exchange_kernel(
    positions, charges, send_table, near_src, near_shift, freq, phase, shift_ops,
    in_bodies, in_rows, harmonic_out, left_out, near_out, moments, bodies,
    r1, r2, r3, l1, l2, l3, opposite,
    singles, doubles, harmonic, left, near, shift, waves, transposed, column_rows, top_rows, row_pack,
    table, tables, table_words, own_table, pair_words, pairs,
    ring_send, ring_recv, small_send, small_recv, plane_send, plane_recv, local_sems, out_sems,
):
    gx, gy = lax.axis_index("gx"), lax.axis_index("gy")
    coarse, fine = row_pack.shape[0], column_rows.shape[0]
    right = {"gy": lax.rem(gy + 1, fine)}
    back = {"gy": lax.rem(gy + fine - 1, fine)}
    half = LEAVES // 2

    def build(quad, carry):
        for member in range(4):
            leaf = quad * 4 + member
            place = pl.ds(pl.multiple_of(leaf * WIDTH, WIDTH), WIDTH)
            bodies[leaf] = jnp.concatenate([positions[:, place], charges[leaf]], axis=0)
        return carry

    lax.fori_loop(0, LEAVES // 4, build, 0)
    table[...] = jnp.zeros_like(table)
    table[: send_table.shape[0], :] = send_table[...]
    barrier = pltpu.get_barrier_semaphore()

    def greet_plane(j, carry):
        pl.semaphore_signal(barrier, inc=1, device_id={"gx": lax.rem(gx + j, coarse)})
        return carry

    lax.fori_loop(1, coarse, greet_plane, 0)
    for k in range(1, fine):
        pl.semaphore_signal(barrier, inc=1, device_id={"gy": lax.rem(gy + k, fine)})
    pl.semaphore_wait(barrier, coarse + fine - 2)

    def remote(source, target, send, recv, device):
        copy = pltpu.make_async_remote_copy(
            src_ref=source, dst_ref=target, send_sem=send, recv_sem=recv, device_id=device
        )
        copy.start()
        return copy

    def ring(step):
        if step == 4:
            return (
                remote(r3.at[pl.ds(0, half)], opposite.at[pl.ds(0, half)],
                       ring_send.at[6], ring_recv.at[6], right),
                remote(l3.at[pl.ds(half, half)], opposite.at[pl.ds(half, half)],
                       ring_send.at[7], ring_recv.at[7], back),
            )
        sources = ((bodies, bodies), (r1, l1), (r2, l2))[step - 1]
        targets = ((r1, l1), (r2, l2), (r3, l3))[step - 1]
        slot = 2 * (step - 1)
        return (
            remote(sources[0], targets[0], ring_send.at[slot], ring_recv.at[slot], right),
            remote(sources[1], targets[1], ring_send.at[slot + 1], ring_recv.at[slot + 1], back),
        )

    for k in range(1, fine):
        there = lax.rem(gy + k, fine)
        remote(table, tables.at[k], small_send.at[0], small_recv.at[0], {"gy": there})
    first = ring(1)
    own_words = pltpu.make_async_copy(table, own_table, local_sems.at[0])
    own_words.start()
    own_words.wait()

    def pack(buffer, position, sources):
        records = 2 * len(sources)
        place = pl.ds((gx * fine + position) * 2, records)

        def one(quad, carry):
            for part in range(4):
                peer = quad * 4 + part
                for number, (block, words) in enumerate(sources):
                    for slot in range(2):
                        buffer[peer, 2 * number + slot] = block[words[slot, peer * fine + gy]]
            return carry

        lax.fori_loop(0, coarse // 4, one, 0)

        def push(j, carry):
            peer = lax.rem(gx + j, coarse)
            remote(buffer.at[peer], in_bodies.at[place], plane_send.at[0], plane_recv.at[0],
                   {"gx": peer})
            return carry

        lax.fori_loop(1, coarse, push, 0)
        keep = pltpu.make_async_copy(buffer.at[gx], in_bodies.at[place], local_sems.at[1 + position])
        keep.start()
        return keep

    kept = [pack(singles.at[0], 0, [(bodies, own_table)])]

    word, taken, _, _ = near_fields(near_src, near_shift)
    pair_words[...] = jnp.zeros_like(pair_words)
    pair_words[:1, :LEAVES] = word[:1].astype(jnp.int32)
    pair_words[1:2, :LEAVES] = jnp.sum(
        jnp.where(taken, word, 0.0), axis=0, keepdims=True
    ).astype(jnp.int32)
    words = pltpu.make_async_copy(pair_words, pairs, local_sems.at[0])
    words.start()
    words.wait()
    pad_into(shift, shift_ops)
    waves[...] = jnp.zeros_like(waves)
    waves[:3, : freq.shape[1]] = freq[...]
    waves[3:4, : freq.shape[1]] = phase[...] * (0.5 / math.pi)
    weights = phase_weights(waves[...])
    lane = lax.broadcasted_iota(jnp.int32, (KPAD, KPAD), 1)
    transposed[...] = jnp.zeros_like(transposed)

    def feature_step(eight, carry):
        for member in range(8):
            leaf = eight * 8 + member
            body = pad8(bodies[leaf])
            basis = basis_leaf(body, weights)
            harmonic[leaf] = basis
            column = jnp.sum(lane_fold(basis * body[3:4]), axis=1, keepdims=True)
            transposed[...] = jnp.where(lane == leaf, column, transposed[...])
            left[leaf, :, :GROUPS] = left_side(body).T.astype(BF16)
        return carry

    def near_step(quad, carry):
        for member in range(4):
            leaf = quad * 4 + member
            sides = []
            for entry in range(2):
                code = pairs[entry, leaf]
                body = pad8(bodies[code & 63])
                charge = body[3:4] * (code >> 21).astype(F32)
                sides.append((source_right(body, (code >> 16) & 31), charge))
            rows = left[leaf][:, :GROUPS]
            for start in range(0, WIDTH, 128):
                near[leaf, start : start + 128] = sum(
                    pair_rows(rows, side, charge, start, 128) for side, charge in sides
                )
        return carry

    left[...] = jnp.zeros_like(left)
    lax.fori_loop(0, half // 8, feature_step, 0)

    first[0].wait_recv()
    first[1].wait_recv()
    second = ring(2)
    sent_tables = tables.at[pl.ds(1, fine - 1)]
    pltpu.make_async_copy(sent_tables, sent_tables, small_recv.at[0]).wait()
    words = pltpu.make_async_copy(
        sent_tables, table_words.at[pl.ds(1, fine - 1)], local_sems.at[0]
    )
    words.start()
    words.wait()
    kept.append(
        pack(doubles.at[0], 1, [(r1, table_words.at[1]), (l1, table_words.at[fine - 1])])
    )
    lax.fori_loop(half // 8, LEAVES // 8, feature_step, 0)

    outs = [
        pltpu.make_async_copy(harmonic, harmonic_out, out_sems.at[0]),
        pltpu.make_async_copy(left, left_out, out_sems.at[1]),
    ]
    for copy in outs:
        copy.start()
    own = transposed[...].T[:LEAVES]
    moments[...] = own
    column_rows[0, :LEAVES] = own
    column_rows[0, LEAVES:] = jnp.broadcast_to(upward(own, shift), (8, KPAD))
    for k in range(1, fine):
        remote(column_rows.at[0], column_rows.at[k], small_send.at[1], small_recv.at[1],
               {"gy": lax.rem(gy + k, fine)})

    second[0].wait_recv()
    second[1].wait_recv()
    third = ring(3)
    kept.append(
        pack(doubles.at[1], 3, [(r2, table_words.at[2]), (l2, table_words.at[fine - 2])])
    )
    lax.fori_loop(0, half // 4, near_step, 0)
    outs.append(
        pltpu.make_async_copy(near.at[pl.ds(0, half)], near_out.at[pl.ds(0, half)], out_sems.at[2])
    )
    outs[-1].start()

    third[0].wait_recv()
    third[1].wait_recv()
    fourth = ring(4)
    kept.append(
        pack(doubles.at[2], 5, [(r3, table_words.at[3]), (l3, table_words.at[fine - 3])])
    )

    others = column_rows.at[pl.ds(1, fine - 1)]
    pltpu.make_async_copy(others, others, small_recv.at[1]).wait()
    for offset in range(fine):
        there = lax.rem(gy + fine - offset, fine)

        def pick(quad, carry):
            for part in range(4):
                peer = quad * 4 + part
                for slot in range(2):
                    row = (table_words.at[offset] if offset else own_table)[
                        slot, peer * fine + gy
                    ]
                    row_pack[peer, pl.ds(there * 2 + slot, 1), :] = column_rows[
                        offset, pl.ds(row, 1), :
                    ]
            return carry

        lax.fori_loop(0, coarse // 4, pick, 0)
        top_rows[pl.ds(there, 1), :] = column_rows[offset, LEAVES : LEAVES + 1, :]

    all_tops = top_rows[...]
    for peer in range(coarse):
        row_pack[peer, 2 * fine :] = all_tops

    def push_rows(j, carry):
        peer = lax.rem(gx + j, coarse)
        remote(row_pack.at[peer], in_rows.at[gx], plane_send.at[1], plane_recv.at[1], {"gx": peer})
        return carry

    lax.fori_loop(1, coarse, push_rows, 0)
    keep = pltpu.make_async_copy(row_pack.at[gx], in_rows.at[gx], local_sems.at[0])
    keep.start()
    kept.append(keep)

    fourth[0].wait_recv()
    fourth[1].wait_recv()
    kept.append(pack(singles.at[1], fine - 1, [(opposite, table_words.at[fine // 2])]))

    lax.fori_loop(half // 4, LEAVES // 4, near_step, 0)
    outs.append(
        pltpu.make_async_copy(
            near.at[pl.ds(half, half)], near_out.at[pl.ds(half, half)], out_sems.at[3]
        )
    )
    outs[-1].start()

    for copy in kept + outs:
        copy.wait()
    for copy in first + second + third + fourth:
        copy.wait_send()
    pltpu.make_async_copy(sent_tables, sent_tables, small_send.at[0]).wait()
    pltpu.make_async_copy(others, others, small_send.at[1]).wait()
    sent = in_bodies.at[pl.ds(0, (coarse - 1) * fine * 2)]
    pltpu.make_async_copy(sent, sent, plane_send.at[0]).wait()
    pltpu.make_async_copy(sent, sent, plane_recv.at[0]).wait()
    sent = in_rows.at[pl.ds(0, coarse - 1)]
    pltpu.make_async_copy(sent, sent, plane_send.at[1]).wait()
    pltpu.make_async_copy(sent, sent, plane_recv.at[1]).wait()


def run_exchange(positions, charges, send_table, near_src, near_shift, freq, phase, shift, coarse, fine):
    block = pltpu.VMEM((LEAVES, 4, WIDTH), F32)
    return pl.pallas_call(
        exchange_kernel,
        out_shape=[
            jax.ShapeDtypeStruct((coarse * fine * 2, 4, WIDTH), F32),
            jax.ShapeDtypeStruct((coarse, 3 * fine, KPAD), F32),
            jax.ShapeDtypeStruct((LEAVES, KPAD, WIDTH), F32),
            jax.ShapeDtypeStruct((LEAVES, WIDTH, 128), BF16),
            jax.ShapeDtypeStruct((LEAVES, WIDTH, 128), F32),
            jax.ShapeDtypeStruct((LEAVES, KPAD), F32),
            jax.ShapeDtypeStruct((LEAVES, 4, WIDTH), F32),
        ],
        in_specs=[VMEM] * 8,
        out_specs=[ANY] * 5 + [VMEM] * 2,
        scratch_shapes=[block] * 7
        + [
            pltpu.VMEM((2, coarse, 2, 4, WIDTH), F32),
            pltpu.VMEM((3, coarse, 4, 4, WIDTH), F32),
            pltpu.VMEM((LEAVES, KPAD, WIDTH), F32),
            pltpu.VMEM((LEAVES, WIDTH, 128), BF16),
            pltpu.VMEM((LEAVES, WIDTH, 128), F32),
            pltpu.VMEM((8, KPAD, KPAD), F32),
            pltpu.VMEM((4, KPAD), F32),
            pltpu.VMEM((KPAD, KPAD), F32),
            pltpu.VMEM((fine, LEAVES + 8, KPAD), F32),
            pltpu.VMEM((fine, KPAD), F32),
            pltpu.VMEM((coarse, 3 * fine, KPAD), F32),
            pltpu.VMEM((8, coarse * fine), jnp.int32),
            pltpu.VMEM((fine, 8, coarse * fine), jnp.int32),
            pltpu.SMEM((fine, 8, coarse * fine), jnp.int32),
            pltpu.SMEM((8, coarse * fine), jnp.int32),
            pltpu.VMEM((8, 128), jnp.int32),
            pltpu.SMEM((8, 128), jnp.int32),
            pltpu.SemaphoreType.DMA((8,)),
            pltpu.SemaphoreType.DMA((8,)),
            pltpu.SemaphoreType.DMA((2,)),
            pltpu.SemaphoreType.DMA((2,)),
            pltpu.SemaphoreType.DMA((2,)),
            pltpu.SemaphoreType.DMA((2,)),
            pltpu.SemaphoreType.DMA((1 + fine,)),
            pltpu.SemaphoreType.DMA((4,)),
        ],
        compiler_params=pltpu.CompilerParams(
            vmem_limit_bytes=62 << 20, collective_id=0, has_side_effects=True
        ),
        cost_estimate=pl.CostEstimate(flops=40_000_000_000, bytes_accessed=60_000_000, transcendentals=0),
    )(positions, charges, send_table, near_src, near_shift, freq, phase, shift)


def local(
    positions,
    charges,
    moment_freq,
    moment_phase,
    m2l_ops,
    child_parent_shift_matrix,
    send_leaf,
    send_count,
    far_src,
    far_class,
    near_src,
    near_shift,
    top_list,
    top_class,
):
    leaves = far_src.shape[0]
    in_bodies, in_rows, harmonic, left, near, moments, bodies = run_exchange(
        positions,
        charges.reshape(leaves, 1, WIDTH),
        send_leaf[0].T,
        near_src.T,
        near_shift.T,
        moment_freq,
        moment_phase[None],
        child_parent_shift_matrix.transpose(1, 0, 2),
        lax.axis_size("gx"),
        lax.axis_size("gy"),
    )
    result = run_finish(
        top_list, top_class, near_src.T, near_shift.T, far_src.T, far_class.T,
        m2l_ops.transpose(1, 0, 2), child_parent_shift_matrix.transpose(1, 0, 2), moments, in_rows,
        left, near, harmonic, bodies, in_bodies,
    )
    return result.reshape(leaves * WIDTH)


def solution(mesh):
    placed = (
        P(None, ("gx", "gy")),
        P(("gx", "gy")),
        P(),
        P(),
        P(),
        P(),
        P(("gx", "gy"), None, None),
        P(("gx", "gy"), None),
        P(("gx", "gy"), None),
        P(("gx", "gy"), None),
        P(("gx", "gy"), None),
        P(("gx", "gy"), None),
        P(("gx", "gy"), None),
        P(("gx", "gy"), None),
    )
    return jax.shard_map(
        local, mesh=mesh, in_specs=placed, out_specs=P(("gx", "gy")), check_vma=False
    )
```

```python
import functools
import math

import jax
import jax.numpy as jnp
from jax import lax
from jax.experimental import pallas as pl
from jax.experimental.pallas import tpu as pltpu
from jax.sharding import PartitionSpec as P

F32 = jnp.float32
BF16 = jnp.bfloat16
SOFTENING = 0.01
LEAVES = 64
WIDTH = 512
KPAD = 128
GROUPS = 48
UNROLL = 8
COS = (1.0, -19.73920440673828, 64.93911743164062, -85.45011138916016, 60.16743087768555, -25.96688461303711, 6.527706146240234)


def split2(a):
    high = a.astype(BF16)
    return high, (a - high.astype(F32)).astype(BF16)


def split3(a):
    high = a.astype(BF16).astype(F32)
    rest = a - high
    middle = rest.astype(BF16).astype(F32)
    return high, middle, rest - middle


def dot_nt(a, b):
    return lax.dot_general(a, b, (((1,), (1,)), ((), ())), preferred_element_type=F32)


def dot_nn(a, b):
    return jnp.dot(a, b, preferred_element_type=F32)


def dot3(dot, a, b):
    a_high, a_low = split2(a)
    b_high, b_low = split2(b)
    return dot(a_high, b_high) + (dot(a_high, b_low) + dot(a_low, b_high))


def pad8(record):
    return jnp.concatenate([record, jnp.zeros((4, record.shape[1]), F32)], axis=0)


def right_side(body, centre):
    row = lax.broadcasted_iota(jnp.int32, body.shape, 0)
    point = jnp.where(row < 3, body - centre, 0.0)
    norm = jnp.sum(point * point, axis=0, keepdims=True) + SOFTENING
    high, middle, low = split3(jnp.where(row == 3, norm, -2.0 * point))
    high_one = jnp.where(row == 3, 1.0, high)
    middle_one = jnp.where(row == 3, 1.0, middle)
    return jnp.concatenate([high, middle, high_one, low, high_one, middle_one], axis=0).astype(BF16)


def left_side(body):
    row = lax.broadcasted_iota(jnp.int32, body.shape, 0)
    point = jnp.where(row < 3, body - 0.5, 0.0)
    norm = jnp.sum(point * point, axis=0, keepdims=True)
    high, middle, low = split3(jnp.where(row == 3, norm, point))
    one = jnp.where(row == 3, 1.0, high)
    return jnp.concatenate(
        [
            one,
            one,
            jnp.where(row == 3, high, middle),
            one,
            jnp.where(row == 3, middle, low),
            jnp.where(row == 3, low, middle),
        ],
        axis=0,
    )


def phase_weights(waves):
    waves = pad8(waves)
    row = lax.broadcasted_iota(jnp.int32, waves.shape, 0)
    freq = jnp.where(row < 3, waves, 0.0)
    turn = jnp.sum(jnp.where(row < 3, 0.5 * waves, waves), axis=0, keepdims=True)
    turn = turn - jnp.round(turn)
    high, middle, low = split3(jnp.where(row == 3, turn, -0.5 * freq))
    plain = jnp.where(row == 3, 0.0, high)
    groups = jnp.concatenate(
        [
            plain,
            plain,
            jnp.where(row == 3, high, middle),
            plain,
            jnp.where(row == 3, middle, low),
            jnp.where(row == 3, low, middle),
        ],
        axis=0,
    )
    return groups.T.astype(BF16)


def cosine_turns(turns):
    rest = turns - jnp.round(turns)
    square = rest * rest
    value = jnp.full_like(square, COS[-1])
    for coefficient in COS[-2::-1]:
        value = value * square + coefficient
    return value


def lane_fold(a):
    return (a[:, :128] + a[:, 128:256]) + (a[:, 256:384] + a[:, 384:])


def basis_leaf(body, weights):
    return cosine_turns(dot_nn(weights, right_side(body, 0.5)))


def upward(moments, shift_ref):
    grouped = moments.reshape(8, 8, KPAD).sum(axis=0)
    row = lax.broadcasted_iota(jnp.int32, grouped.shape, 0)
    total = jnp.zeros((8, KPAD), F32)
    for child in range(8):
        total = total + dot3(dot_nt, jnp.where(row == child, grouped, 0.0), shift_ref[child])
    return jnp.sum(total, axis=0, keepdims=True)


def offset_vector(code):
    return (
        (code % 3 - 1).astype(F32),
        (code // 3 % 3 - 1).astype(F32),
        (code // 9 - 1).astype(F32),
    )


def source_right(body, shift):
    row = lax.broadcasted_iota(jnp.int32, body.shape, 0)
    shift_x, shift_y, shift_z = offset_vector(shift)
    centre = 0.5 - jnp.where(row == 0, shift_x, jnp.where(row == 1, shift_y, shift_z))
    return right_side(body, centre)


def pair_rows(left, right, charge, start, size):
    value = charge * lax.rsqrt(dot_nn(left[start : start + size], right))
    return lane_fold(value)


def near_fields(near_src, near_shift):
    source = near_src[...]
    column = lax.broadcasted_iota(jnp.int32, source.shape, 0)
    own = (source >= 0) & (source < LEAVES) & (column > 0)
    first_own = jnp.min(jnp.where(own, column.astype(F32), 8.0), axis=0, keepdims=True)
    taken = column.astype(F32) == first_own
    wanted = (source >= 0) & (column > 0) & jnp.logical_not(taken)
    word = (source + near_shift[...] * 65536 + (1 << 21)).astype(F32)
    return word, taken, wanted, source


def near_list(near_src, near_shift, listed):
    word, _, wanted, source = near_fields(near_src, near_shift)
    lane = lax.broadcasted_iota(jnp.int32, source.shape, 1)
    slot = source - LEAVES
    back = (lax.axis_index("gy") - (slot >> 1)) & 7
    position = jnp.where(
        back == 0, 0, jnp.where(back < 4, 2 * back - 1, jnp.where(back == 4, 7, 16 - 2 * back))
    )
    place = jnp.where(slot < 0, source, LEAVES + (slot >> 4) * 16 + position * 2 + (slot & 1))
    word = word + (place * 64 - source + lane).astype(F32)
    mark = jnp.where(wanted, 1.0, 0.0)
    first = lax.broadcasted_iota(jnp.int32, (LEAVES, LEAVES), 0)
    second = lax.broadcasted_iota(jnp.int32, (LEAVES, LEAVES), 1)
    same = (first >> 5) == (second >> 5)
    before = jnp.where(same & (first < second), 1.0, 0.0).astype(BF16)
    rank = dot_nn(mark.astype(BF16), before)
    totals = dot_nn(mark.astype(BF16), jnp.where(same, 1.0, 0.0).astype(BF16))
    row = lax.broadcasted_iota(jnp.int32, (8, LEAVES), 0)
    for column in range(8):
        rank = rank + jnp.where(row > column, totals[column : column + 1], 0.0)
    rank = rank.astype(jnp.int32) + (lane >> 5) * 256
    rank = jnp.where(wanted, rank, -1)
    parts = split3(word)
    codes = jnp.zeros((8, LEAVES), F32)
    for column in range(8):
        at = rank[column : column + 1]
        low = jnp.where(first == (at & 63), 1.0, 0.0).astype(BF16)
        for part in parts:
            high = jnp.where(row == (at >> 6), part[column : column + 1], 0.0).astype(BF16)
            codes = codes + dot_nt(high, low)
    number = jnp.broadcast_to(jnp.sum(totals, axis=0, keepdims=True), (8, LEAVES))
    listed[...] = jnp.concatenate([codes, number], axis=1).astype(jnp.int32)


def pad_into(padded, ops):
    size, classes, width = ops.shape
    flat = ops.reshape(size * classes, width)
    padded[...] = jnp.zeros_like(padded)
    for place in range(classes):
        padded[place, :size, :width] = flat[pl.ds(place, size, stride=classes), :]


def local_expansions(pool_moments, m2l, shift, table, far_index, top_class, expansions):
    rows = pool_moments.shape[0]
    pool_high, pool_low = split2(pool_moments[...])
    for pair in range(8):
        op_high, op_low = split2(m2l[2 * pair : 2 * pair + 2].reshape(256, KPAD))
        moved = dot_nt(pool_high, op_high) + (dot_nt(pool_high, op_low) + dot_nt(pool_low, op_high))
        table[2 * pair * rows : (2 * pair + 1) * rows] = moved[:, :KPAD]
        table[(2 * pair + 1) * rows : (2 * pair + 2) * rows] = moved[:, KPAD:]
    table[16 * rows : 16 * rows + 8] = jnp.zeros((8, KPAD), F32)

    def tree(parts):
        while len(parts) > 1:
            parts = [a + b for a, b in zip(parts[::2], parts[1::2])]
        return parts[0]

    top_local = tree(
        [table[pl.ds(top_class[0, e] * rows + (rows - 32 + e), 1), :] for e in range(32)]
    )
    top_rows = jnp.broadcast_to(top_local, (8, KPAD))
    row = lax.broadcasted_iota(jnp.int32, (8, KPAD), 0)
    down = jnp.zeros((8, KPAD), F32)
    for child in range(8):
        down = jnp.where(row == child, dot3(dot_nn, top_rows, shift[child]), down)

    def gather(leaf, carry):
        expansions[pl.ds(leaf, 1), :] = tree(
            [table[pl.ds(far_index[e, leaf], 1), :] for e in range(32)]
        )
        return carry

    lax.fori_loop(0, LEAVES, gather, 0)
    return (expansions[...].reshape(8, 8, KPAD) + down[None]).reshape(LEAVES, KPAD)


def finish_kernel(
    top_list, top_class,
    near_src, near_shift, far_src, far_class, m2l_ops, shift_ops, own_moments, in_rows,
    left_hbm, near_hbm, harmonic_hbm, bodies_hbm, in_bodies_hbm,
    out,
    pool, left, near, harmonic, pool_moments, table, expansions, m2l, shift,
    listed, far_rows, codes, far_index, sems,
):
    slots = in_bodies_hbm.shape[0]
    copies = [
        pltpu.make_async_copy(source, target, sems.at[place])
        for place, (source, target) in enumerate(
            (
                (left_hbm, left),
                (bodies_hbm, pool.at[pl.ds(0, LEAVES)]),
                (in_bodies_hbm, pool.at[pl.ds(LEAVES, slots)]),
                (near_hbm.at[pl.ds(0, LEAVES // 2)], near.at[pl.ds(0, LEAVES // 2)]),
                (
                    near_hbm.at[pl.ds(LEAVES // 2, LEAVES // 2)],
                    near.at[pl.ds(LEAVES // 2, LEAVES // 2)],
                ),
                (harmonic_hbm, harmonic),
            )
        )
    ]
    for copy in copies:
        copy.start()
    entry_rows = 16 * (LEAVES + slots + 32)
    source = far_src[...]
    far_rows[...] = jnp.zeros_like(far_rows)
    far_rows[:, :LEAVES] = jnp.where(
        source >= 0, far_class[...] * (entry_rows // 16) + source, entry_rows
    )
    near_list(near_src, near_shift, listed)
    words = [
        pltpu.make_async_copy(far_rows, far_index, sems.at[6]),
        pltpu.make_async_copy(listed, codes, sems.at[7]),
    ]
    for copy in words:
        copy.start()
    pad_into(m2l, m2l_ops)
    pad_into(shift, shift_ops)
    rows = LEAVES + slots
    pool_moments[:LEAVES] = own_moments[...]
    fine = in_rows.shape[1] // 3
    for peer in range(in_rows.shape[0]):
        start = LEAVES + 2 * fine * peer
        pool_moments[start : start + 2 * fine] = in_rows[peer, : 2 * fine]
    for e in range(32):
        owner = top_list[0, e]
        pool_moments[rows + e : rows + e + 1, :] = in_rows[
            owner // fine, pl.ds(2 * fine + lax.rem(owner, fine), 1), :
        ]
    for copy in words:
        copy.wait()
    local = local_expansions(pool_moments, m2l, shift, table, far_index, top_class, expansions)
    local_columns = jnp.concatenate([local, jnp.zeros((KPAD - LEAVES, KPAD), F32)], axis=0).T

    for copy in copies[:4]:
        copy.wait()

    def near_step(group, half):
        for member in range(UNROLL):
            code = codes[4 * half + (group >> 3), (group & 7) * UNROLL + member]
            target = code & 63
            source = (code >> 6) & 1023
            live = (code >> 21).astype(F32)
            body = pad8(pool[source])
            right = source_right(body, (code >> 16) & 31)
            charge = body[3:4] * live
            for start in range(0, WIDTH, 128):
                near[target, start : start + 128] += pair_rows(
                    left.at[target][:, :GROUPS], right, charge, start, 128
                )
        return half

    lax.fori_loop(0, (codes[0, LEAVES] + UNROLL - 1) // UNROLL, near_step, 0)
    copies[4].wait()
    lax.fori_loop(0, (codes[0, LEAVES + 32] + UNROLL - 1) // UNROLL, near_step, 1)
    copies[5].wait()
    ones = jnp.ones((8, 128), BF16)

    def far_step(group, columns):
        for member in range(8):
            leaf = group * 8 + member
            product = harmonic[leaf] * columns[:, member : member + 1]
            far = jnp.sum(product, axis=0, keepdims=True)
            near_high, near_low = split2(near[leaf])
            total = dot_nt(ones, near_high) + dot_nt(ones, near_low)
            out[leaf] = total[:1] + far
        return pltpu.roll(columns, KPAD - 8, 1)

    lax.fori_loop(0, LEAVES // 8, far_step, local_columns)


SMEM = pl.BlockSpec(memory_space=pltpu.SMEM)
VMEM = pl.BlockSpec(memory_space=pltpu.VMEM)
ANY = pl.BlockSpec(memory_space=pl.ANY)


def run_finish(
    top_list, top_class, near_src, near_shift, far_src, far_class, m2l, shift, moments, in_rows,
    left, near, harmonic, bodies, in_bodies,
):
    slots = in_bodies.shape[0]
    rows = LEAVES + slots + 32
    return pl.pallas_call(
        finish_kernel,
        out_shape=jax.ShapeDtypeStruct((LEAVES, 1, WIDTH), F32),
        in_specs=[SMEM] * 2 + [VMEM] * 8 + [ANY] * 5,
        out_specs=VMEM,
        scratch_shapes=[
            pltpu.VMEM((LEAVES + slots, 4, WIDTH), F32),
            pltpu.VMEM((LEAVES, WIDTH, 128), BF16),
            pltpu.VMEM((LEAVES, WIDTH, 128), F32),
            pltpu.VMEM((LEAVES, KPAD, WIDTH), F32),
            pltpu.VMEM((rows, KPAD), F32),
            pltpu.VMEM((16 * rows + 8, KPAD), F32),
            pltpu.VMEM((LEAVES, KPAD), F32),
            pltpu.VMEM((16, KPAD, KPAD), F32),
            pltpu.VMEM((8, KPAD, KPAD), F32),
            pltpu.VMEM((8, 128), jnp.int32),
            pltpu.VMEM((32, 128), jnp.int32),
            pltpu.SMEM((8, 128), jnp.int32),
            pltpu.SMEM((32, 128), jnp.int32),
            pltpu.SemaphoreType.DMA((8,)),
        ],
        compiler_params=pltpu.CompilerParams(vmem_limit_bytes=62 << 20),
        cost_estimate=pl.CostEstimate(flops=60_000_000_000, bytes_accessed=40_000_000, transcendentals=0),
    )(
        top_list, top_class, near_src, near_shift, far_src, far_class, m2l, shift, moments, in_rows,
        left, near, harmonic, bodies, in_bodies,
    )


def exchange_kernel(
    positions, charges, send_table, near_src, near_shift, freq, phase, shift_ops,
    in_bodies, in_rows, harmonic_out, left_out, near_out, moments, bodies,
    r1, r2, r3, l1, l2, l3, opposite,
    singles, doubles, harmonic, left, near, shift, waves, transposed, column_rows, top_rows, row_pack,
    table, tables, table_words, own_table, pair_words, pairs,
    ring_send, ring_recv, small_send, small_recv, plane_send, plane_recv, local_sems, out_sems,
):
    gx, gy = lax.axis_index("gx"), lax.axis_index("gy")
    coarse, fine = row_pack.shape[0], column_rows.shape[0]
    right = {"gy": lax.rem(gy + 1, fine)}
    back = {"gy": lax.rem(gy + fine - 1, fine)}
    half = LEAVES // 2

    def build(quad, carry):
        for member in range(4):
            leaf = quad * 4 + member
            place = pl.ds(pl.multiple_of(leaf * WIDTH, WIDTH), WIDTH)
            bodies[leaf] = jnp.concatenate([positions[:, place], charges[leaf]], axis=0)
        return carry

    lax.fori_loop(0, LEAVES // 4, build, 0)
    table[...] = jnp.zeros_like(table)
    table[: send_table.shape[0], :] = send_table[...]
    barrier = pltpu.get_barrier_semaphore()

    def greet_plane(j, carry):
        pl.semaphore_signal(barrier, inc=1, device_id={"gx": lax.rem(gx + j, coarse)})
        return carry

    lax.fori_loop(1, coarse, greet_plane, 0)
    for k in range(1, fine):
        pl.semaphore_signal(barrier, inc=1, device_id={"gy": lax.rem(gy + k, fine)})
    pl.semaphore_wait(barrier, coarse + fine - 2)

    def remote(source, target, send, recv, device):
        copy = pltpu.make_async_remote_copy(
            src_ref=source, dst_ref=target, send_sem=send, recv_sem=recv, device_id=device
        )
        copy.start()
        return copy

    def ring(step):
        if step == 4:
            return (
                remote(r3.at[pl.ds(0, half)], opposite.at[pl.ds(0, half)],
                       ring_send.at[6], ring_recv.at[6], right),
                remote(l3.at[pl.ds(half, half)], opposite.at[pl.ds(half, half)],
                       ring_send.at[7], ring_recv.at[7], back),
            )
        sources = ((bodies, bodies), (r1, l1), (r2, l2))[step - 1]
        targets = ((r1, l1), (r2, l2), (r3, l3))[step - 1]
        slot = 2 * (step - 1)
        return (
            remote(sources[0], targets[0], ring_send.at[slot], ring_recv.at[slot], right),
            remote(sources[1], targets[1], ring_send.at[slot + 1], ring_recv.at[slot + 1], back),
        )

    for k in range(1, fine):
        there = lax.rem(gy + k, fine)
        remote(table, tables.at[k], small_send.at[0], small_recv.at[0], {"gy": there})
    first = ring(1)
    own_words = pltpu.make_async_copy(table, own_table, local_sems.at[0])
    own_words.start()
    own_words.wait()

    def pack(buffer, position, sources):
        records = 2 * len(sources)
        place = pl.ds((gx * fine + position) * 2, records)

        def one(quad, carry):
            for part in range(4):
                peer = quad * 4 + part
                for number, (block, words) in enumerate(sources):
                    for slot in range(2):
                        buffer[peer, 2 * number + slot] = block[words[slot, peer * fine + gy]]
            return carry

        lax.fori_loop(0, coarse // 4, one, 0)

        def push(j, carry):
            peer = lax.rem(gx + j, coarse)
            remote(buffer.at[peer], in_bodies.at[place], plane_send.at[0], plane_recv.at[0],
                   {"gx": peer})
            return carry

        lax.fori_loop(1, coarse, push, 0)
        keep = pltpu.make_async_copy(buffer.at[gx], in_bodies.at[place], local_sems.at[1 + position])
        keep.start()
        return keep

    kept = [pack(singles.at[0], 0, [(bodies, own_table)])]

    word, taken, _, _ = near_fields(near_src, near_shift)
    pair_words[...] = jnp.zeros_like(pair_words)
    pair_words[:1, :LEAVES] = word[:1].astype(jnp.int32)
    pair_words[1:2, :LEAVES] = jnp.sum(
        jnp.where(taken, word, 0.0), axis=0, keepdims=True
    ).astype(jnp.int32)
    words = pltpu.make_async_copy(pair_words, pairs, local_sems.at[0])
    words.start()
    words.wait()
    pad_into(shift, shift_ops)
    waves[...] = jnp.zeros_like(waves)
    waves[:3, : freq.shape[1]] = freq[...]
    waves[3:4, : freq.shape[1]] = phase[...] * (0.5 / math.pi)
    weights = phase_weights(waves[...])
    lane = lax.broadcasted_iota(jnp.int32, (KPAD, KPAD), 1)
    transposed[...] = jnp.zeros_like(transposed)

    def feature_step(eight, carry):
        for member in range(8):
            leaf = eight * 8 + member
            body = pad8(bodies[leaf])
            basis = basis_leaf(body, weights)
            harmonic[leaf] = basis
            column = jnp.sum(lane_fold(basis * body[3:4]), axis=1, keepdims=True)
            transposed[...] = jnp.where(lane == leaf, column, transposed[...])
            left[leaf, :, :GROUPS] = left_side(body).T.astype(BF16)
        return carry

    def near_step(quad, carry):
        for member in range(4):
            leaf = quad * 4 + member
            sides = []
            for entry in range(2):
                code = pairs[entry, leaf]
                body = pad8(bodies[code & 63])
                charge = body[3:4] * (code >> 21).astype(F32)
                sides.append((source_right(body, (code >> 16) & 31), charge))
            rows = left[leaf][:, :GROUPS]
            for start in range(0, WIDTH, 128):
                near[leaf, start : start + 128] = sum(
                    pair_rows(rows, side, charge, start, 128) for side, charge in sides
                )
        return carry

    def near_away(start, stop, place):
        rows = pl.ds(start, stop - start)
        outs.append(pltpu.make_async_copy(near.at[rows], near_out.at[rows], out_sems.at[place]))
        outs[-1].start()

    left[...] = jnp.zeros_like(left)
    lax.fori_loop(0, half // 8, feature_step, 0)

    first[0].wait_recv()
    first[1].wait_recv()
    second = ring(2)
    sent_tables = tables.at[pl.ds(1, fine - 1)]
    pltpu.make_async_copy(sent_tables, sent_tables, small_recv.at[0]).wait()
    words = pltpu.make_async_copy(
        sent_tables, table_words.at[pl.ds(1, fine - 1)], local_sems.at[0]
    )
    words.start()
    words.wait()
    kept.append(
        pack(doubles.at[0], 1, [(r1, table_words.at[1]), (l1, table_words.at[fine - 1])])
    )
    lax.fori_loop(half // 8, LEAVES // 8 - 1, feature_step, 0)

    second[0].wait_recv()
    second[1].wait_recv()
    third = ring(3)
    kept.append(
        pack(doubles.at[1], 3, [(r2, table_words.at[2]), (l2, table_words.at[fine - 2])])
    )
    lax.fori_loop(LEAVES // 8 - 1, LEAVES // 8, feature_step, 0)

    outs = [
        pltpu.make_async_copy(harmonic, harmonic_out, out_sems.at[0]),
        pltpu.make_async_copy(left, left_out, out_sems.at[1]),
    ]
    for copy in outs:
        copy.start()
    own = transposed[...].T[:LEAVES]
    moments[...] = own
    column_rows[0, :LEAVES] = own
    column_rows[0, LEAVES:] = jnp.broadcast_to(upward(own, shift), (8, KPAD))
    for k in range(1, fine):
        remote(column_rows.at[0], column_rows.at[k], small_send.at[1], small_recv.at[1],
               {"gy": lax.rem(gy + k, fine)})

    lax.fori_loop(0, 4, near_step, 0)

    third[0].wait_recv()
    third[1].wait_recv()
    fourth = ring(4)
    kept.append(
        pack(doubles.at[2], 5, [(r3, table_words.at[3]), (l3, table_words.at[fine - 3])])
    )

    lax.fori_loop(4, 6, near_step, 0)
    near_away(0, 24, 2)

    fourth[0].wait_recv()
    fourth[1].wait_recv()
    kept.append(pack(singles.at[1], fine - 1, [(opposite, table_words.at[fine // 2])]))

    others = column_rows.at[pl.ds(1, fine - 1)]
    pltpu.make_async_copy(others, others, small_recv.at[1]).wait()
    for offset in range(fine):
        there = lax.rem(gy + fine - offset, fine)

        def pick(quad, carry):
            for part in range(4):
                peer = quad * 4 + part
                for slot in range(2):
                    row = (table_words.at[offset] if offset else own_table)[
                        slot, peer * fine + gy
                    ]
                    row_pack[peer, pl.ds(there * 2 + slot, 1), :] = column_rows[
                        offset, pl.ds(row, 1), :
                    ]
            return carry

        lax.fori_loop(0, coarse // 4, pick, 0)
        top_rows[pl.ds(there, 1), :] = column_rows[offset, LEAVES : LEAVES + 1, :]

    all_tops = top_rows[...]
    for peer in range(coarse):
        row_pack[peer, 2 * fine :] = all_tops

    def push_rows(j, carry):
        peer = lax.rem(gx + j, coarse)
        remote(row_pack.at[peer], in_rows.at[gx], plane_send.at[1], plane_recv.at[1], {"gx": peer})
        return carry

    lax.fori_loop(1, coarse, push_rows, 0)
    keep = pltpu.make_async_copy(row_pack.at[gx], in_rows.at[gx], local_sems.at[0])
    keep.start()
    kept.append(keep)

    lax.fori_loop(6, 11, near_step, 0)
    near_away(24, 44, 3)
    lax.fori_loop(11, LEAVES // 4, near_step, 0)
    near_away(44, LEAVES, 4)

    for copy in kept + outs:
        copy.wait()
    for copy in first + second + third + fourth:
        copy.wait_send()
    pltpu.make_async_copy(sent_tables, sent_tables, small_send.at[0]).wait()
    pltpu.make_async_copy(others, others, small_send.at[1]).wait()
    sent = in_bodies.at[pl.ds(0, (coarse - 1) * fine * 2)]
    pltpu.make_async_copy(sent, sent, plane_send.at[0]).wait()
    pltpu.make_async_copy(sent, sent, plane_recv.at[0]).wait()
    sent = in_rows.at[pl.ds(0, coarse - 1)]
    pltpu.make_async_copy(sent, sent, plane_send.at[1]).wait()
    pltpu.make_async_copy(sent, sent, plane_recv.at[1]).wait()


def run_exchange(positions, charges, send_table, near_src, near_shift, freq, phase, shift, coarse, fine):
    block = pltpu.VMEM((LEAVES, 4, WIDTH), F32)
    return pl.pallas_call(
        exchange_kernel,
        out_shape=[
            jax.ShapeDtypeStruct((coarse * fine * 2, 4, WIDTH), F32),
            jax.ShapeDtypeStruct((coarse, 3 * fine, KPAD), F32),
            jax.ShapeDtypeStruct((LEAVES, KPAD, WIDTH), F32),
            jax.ShapeDtypeStruct((LEAVES, WIDTH, 128), BF16),
            jax.ShapeDtypeStruct((LEAVES, WIDTH, 128), F32),
            jax.ShapeDtypeStruct((LEAVES, KPAD), F32),
            jax.ShapeDtypeStruct((LEAVES, 4, WIDTH), F32),
        ],
        in_specs=[VMEM] * 8,
        out_specs=[ANY] * 5 + [VMEM] * 2,
        scratch_shapes=[block] * 7
        + [
            pltpu.VMEM((2, coarse, 2, 4, WIDTH), F32),
            pltpu.VMEM((3, coarse, 4, 4, WIDTH), F32),
            pltpu.VMEM((LEAVES, KPAD, WIDTH), F32),
            pltpu.VMEM((LEAVES, WIDTH, 128), BF16),
            pltpu.VMEM((LEAVES, WIDTH, 128), F32),
            pltpu.VMEM((8, KPAD, KPAD), F32),
            pltpu.VMEM((4, KPAD), F32),
            pltpu.VMEM((KPAD, KPAD), F32),
            pltpu.VMEM((fine, LEAVES + 8, KPAD), F32),
            pltpu.VMEM((fine, KPAD), F32),
            pltpu.VMEM((coarse, 3 * fine, KPAD), F32),
            pltpu.VMEM((8, coarse * fine), jnp.int32),
            pltpu.VMEM((fine, 8, coarse * fine), jnp.int32),
            pltpu.SMEM((fine, 8, coarse * fine), jnp.int32),
            pltpu.SMEM((8, coarse * fine), jnp.int32),
            pltpu.VMEM((8, 128), jnp.int32),
            pltpu.SMEM((8, 128), jnp.int32),
            pltpu.SemaphoreType.DMA((8,)),
            pltpu.SemaphoreType.DMA((8,)),
            pltpu.SemaphoreType.DMA((2,)),
            pltpu.SemaphoreType.DMA((2,)),
            pltpu.SemaphoreType.DMA((2,)),
            pltpu.SemaphoreType.DMA((2,)),
            pltpu.SemaphoreType.DMA((1 + fine,)),
            pltpu.SemaphoreType.DMA((5,)),
        ],
        compiler_params=pltpu.CompilerParams(
            vmem_limit_bytes=62 << 20, collective_id=0, has_side_effects=True
        ),
        cost_estimate=pl.CostEstimate(flops=40_000_000_000, bytes_accessed=60_000_000, transcendentals=0),
    )(positions, charges, send_table, near_src, near_shift, freq, phase, shift)


def local(
    positions,
    charges,
    moment_freq,
    moment_phase,
    m2l_ops,
    child_parent_shift_matrix,
    send_leaf,
    send_count,
    far_src,
    far_class,
    near_src,
    near_shift,
    top_list,
    top_class,
):
    leaves = far_src.shape[0]
    in_bodies, in_rows, harmonic, left, near, moments, bodies = run_exchange(
        positions,
        charges.reshape(leaves, 1, WIDTH),
        send_leaf[0].T,
        near_src.T,
        near_shift.T,
        moment_freq,
        moment_phase[None],
        child_parent_shift_matrix.transpose(1, 0, 2),
        lax.axis_size("gx"),
        lax.axis_size("gy"),
    )
    result = run_finish(
        top_list, top_class, near_src.T, near_shift.T, far_src.T, far_class.T,
        m2l_ops.transpose(1, 0, 2), child_parent_shift_matrix.transpose(1, 0, 2), moments, in_rows,
        left, near, harmonic, bodies, in_bodies,
    )
    return result.reshape(leaves * WIDTH)


def solution(mesh):
    placed = (
        P(None, ("gx", "gy")),
        P(("gx", "gy")),
        P(),
        P(),
        P(),
        P(),
        P(("gx", "gy"), None, None),
        P(("gx", "gy"), None),
        P(("gx", "gy"), None),
        P(("gx", "gy"), None),
        P(("gx", "gy"), None),
        P(("gx", "gy"), None),
        P(("gx", "gy"), None),
        P(("gx", "gy"), None),
    )
    return jax.shard_map(
        local, mesh=mesh, in_specs=placed, out_specs=P(("gx", "gy")), check_vma=False
    )
```
